32 devices in a mesh: depth: 2 (over x), lat: 16 (over z, y, core).
Axes of the slice: x: 2, y: 2, z: 4, core: 2. Of those that a mesh axis runs over, the one named last changes fastest.
Arguments:
- fem_disp: float32 [3, 8, 128, 256], P(None, 'depth', 'lat'), may hold values from -6 to 6
- fem_vel: float32 [3, 8, 128, 256], P(None, 'depth', 'lat'), may hold values from -6 to 6
- modulus: float32 [8, 128, 256], P('depth', 'lat'), may hold values from 0.5 to 5
- inv_mass: float32 [8, 128, 256], P('depth', 'lat'), may hold values from 0.5 to 2
- element_stiffness: float32 [24, 24], replicated, may hold values from -1.25 to 1.25
- pd_pos: float32 [3, 65536], P(None, ('depth', 'lat')), may hold values from -4 to 4
- pd_disp: float32 [3, 65536], P(None, ('depth', 'lat')), may hold values from -6 to 6
- pd_vel: float32 [3, 65536], P(None, ('depth', 'lat')), may hold values from -6 to 6
- conv_state: float32 [9, 2048], P(None, ('depth', 'lat')), may hold values from -5 to 5
- conv_owner: int32 [2048, 1], P(('depth', 'lat')), may hold values from 0 to 15; in each aligned block of 64 rows (0 to 63, 64 to 127, ...) at most 8 rows name the same one
- family: int32 [544, 8], P(('depth', 'lat')), may hold values from 0 to 51
- ov_owner: int32 [2048, 1], P(('depth', 'lat')), may hold values from 0 to 15; in each aligned block of 64 rows (0 to 63, 64 to 127, ...) at most 8 rows name the same one
- ov_node: int32 [2048], P(('depth', 'lat')), may hold values from 0 to 8191
- ov_target: int32 [2048], P(('depth', 'lat')), may hold values from 0 to 2047
- ov_stiff: float32 [2048], P(('depth', 'lat')), may hold values from 0.5 to 4
Outputs:
- fem_vel_new: float32 [3, 8, 128, 256], P(None, 'depth', 'lat')
- pd_vel_new: float32 [3, 69632], P(None, ('depth', 'lat'))
The draws below stay inside these ranges and needn't reach their ends.
Inputs may be any that keep to these rules, and one draw needn't show every extreme that they name: `conv_owner`: among the 64 rows of one device at most 8 name the same owner, and some owner gets exactly 8 of them. `ov_owner`: among the 64 entries of one device at most 8 name the same owner, and some owner gets exactly 8 of them. `family`: values below 17 number blocks of the previous lat index's table, the next 17 the device's own, the next 17 the following lat index's; 51 is the empty block.
All inputs are finite; a program needn't handle non-finite values.
Results may differ from the reference program's by a relative error of at most 0.0003.
Values sent between devices are 32-bit elements; how exact they have to be, the bound alone decides.
No kernel may reach another device: no remote copies, remote signals or barrier semaphores. Data moves between devices by JAX's collectives and lax.ppermute only.
A program may use at most 64 MiB of HBM per device.

```python
import math
import jax
import jax.numpy as jnp
import numpy as np
from jax import lax

NX = 4
NY = 8
NZ = 256
P_OWN = 2048
BLOCK = 128
FAM = 8
CAP = 8
OCAP = 8
CONV_DEV = 64
OV_DEV = 64
TAIL = 128
P_DEV = 2176
NBT = 17
GX = 8
GY = 128
PD_OWN_TOTAL = 65536
PD_TOTAL = 69632
CONV_TOTAL = 2048
OV_TOTAL = 2048
N_DEPTH = 2
N_LAT = 16
DEVICES = 32


def touch_ends(values, key, low, top_value):
    extent = values.shape
    spot = [jax.random.randint(jax.random.fold_in(key, axis), (), 0, extent[axis]) for axis in range(len(extent))]
    values = values.at[tuple(spot)].set(low)
    longest = extent.index(max(extent))
    spot[longest] = (spot[longest] + 1) % extent[longest]
    return values.at[tuple(spot)].set(top_value)


def block_scale(rng, shape, cuts, low, high):
    def one(position, parts):
        steps = jax.random.uniform(jax.random.fold_in(jax.random.fold_in(rng, 6), position), (parts,), jnp.float32, low / len(cuts), high / len(cuts))
        return jnp.repeat(jnp.exp(steps), shape[position] // parts).reshape((-1,) + (1,) * (len(shape) - position - 1))

    gain = one(*cuts[0])
    for cut in cuts[1:]:
        gain = gain * one(*cut)
    return gain


def deal_out(rng, own, number, rows, amount, top, limit, slope):
    order = jax.random.permutation(rng, amount)
    packed, ordinary = load_shares(amount, rows * top, limit, slope, True), load_shares(amount, rows * top, limit, slope, False)
    places = jnp.arange(amount)

    def named(sizes, offset_by):
        used = int((sizes > 0).sum())
        fixed = max(1, used // 4)
        passed = fixed + (places - fixed + offset_by * (used - fixed)) % max(1, amount - fixed)
        return jnp.zeros((amount,), jnp.int32).at[order[jnp.where(places < fixed, places, passed)]].set(jnp.asarray(sizes, jnp.int32))

    sizes = jnp.where(number % 4 == 0, named(packed, number // 4), named(ordinary, number - number // 4 - 1))
    mixed = jax.random.permutation(jax.random.fold_in(own, 3), amount)
    donor, taker = mixed[0:amount // 2 * 2:2], mixed[1:amount // 2 * 2:2]
    room = jnp.minimum(sizes[donor] - 1, limit - sizes[taker]) // 2
    room = jnp.where((donor == order[0]) | (taker == order[0]) | (sizes[taker] == 0), 0, jnp.maximum(room, 0))
    passed = jax.random.randint(jax.random.fold_in(own, 4), (amount // 2,), 0, 1 << 20) % (room + 1)
    sizes = sizes.at[donor].add(-passed).at[taker].add(passed)
    items = jnp.searchsorted(jnp.cumsum(sizes), jnp.arange(rows * top), side="right").astype(jnp.int32)
    table = items.reshape(top, rows).T
    table = table[jax.random.permutation(jax.random.fold_in(own, 1), rows)]
    offset_by = jax.random.randint(jax.random.fold_in(own, 2), (rows, 1), 0, top)
    return jnp.take_along_axis(table, (jnp.arange(top)[None, :] + offset_by) % top, axis=1)


def load_shares(amount, total, reach, skew, full):
    portions = [(1 << 20) // math.isqrt(rank ** skew) + 1 for rank in range(1, amount + 1)]
    largest = reach if full else min(reach, max(-(-total // amount), total * portions[0] // sum(portions)))
    least = 1 if total - largest >= amount - 1 else 0
    counts, spare = [largest] + [least] * (amount - 1), total - largest - least * (amount - 1)
    while spare > 0:
        free = [i for i in range(1, amount) if counts[i] < largest] or [i for i in range(1, amount) if counts[i] < reach]
        whole, left = sum([portions[i] for i in free]), spare
        for i in free:
            more = min(reach - counts[i], max(1, left * portions[i] // whole), spare)
            counts[i] = counts[i] + more
            spare = spare - more
    return np.array(counts)


def bell_draw(stream_key, dims, scale, most, pieces=(), kind=jnp.bfloat16):
    result = scale * jax.random.normal(stream_key, dims, jnp.float32)
    if pieces:
        result = result * block_scale(stream_key, dims, pieces, -0.22, 0.18)
    return jnp.clip(result, -most, most).astype(kind)


def setup_inputs(seed: int = 0) -> dict:
    splits = jax.random.split(jax.random.key(seed), 16)
    fem_disp = bell_draw(splits[0], (3, GX, GY, NZ), 1.0, 6.0, ((1, 2), (2, 16)), jnp.float32)
    fem_vel = bell_draw(splits[1], (3, GX, GY, NZ), 1.0, 6.0, ((1, 2), (2, 16)), jnp.float32)
    modulus = jnp.clip(jnp.exp(math.log(5.0) - 2.3025851 * jax.random.uniform(splits[2], (GX, GY, NZ), jnp.float32) ** block_scale(splits[2], (GX, GY, NZ), ((0, 2), (1, 16)), -0.2, 0.2)), 0.5, 5.0)
    inv_mass = jnp.clip(jnp.exp(math.log(2.0) - 1.3862944 * jax.random.uniform(splits[3], (GX, GY, NZ), jnp.float32) ** block_scale(splits[3], (GX, GY, NZ), ((0, 2), (1, 16)), -0.2, 0.2)), 0.5, 2.0)
    element_stiffness = bell_draw(splits[4], (24, 24), 24 ** -0.5, 1.25, (), jnp.float32)
    pd_pos = bell_draw(splits[5], (3, PD_OWN_TOTAL), 0.8, 4.0, ((1, 32),), jnp.float32)
    pd_disp = bell_draw(splits[6], (3, PD_OWN_TOTAL), 1.0, 6.0, ((1, 32),), jnp.float32)
    pd_vel = bell_draw(splits[7], (3, PD_OWN_TOTAL), 1.0, 6.0, ((1, 32),), jnp.float32)
    conv_state = bell_draw(splits[8], (9, CONV_TOTAL), 0.8, 5.0, ((1, 32),), jnp.float32)
    conv_owner_keys = jax.random.split(jax.random.fold_in(splits[9], 1), CONV_TOTAL // CONV_DEV)
    conv_owner_turns = jax.random.permutation(jax.random.fold_in(splits[9], 3), CONV_TOTAL // CONV_DEV)
    conv_owner = jax.vmap(lambda own, number: deal_out(jax.random.fold_in(splits[9], 2), own, number, CONV_DEV, N_LAT, 1, CAP, 2))(conv_owner_keys, conv_owner_turns).reshape((CONV_TOTAL, 1))
    family = touch_ends(jax.random.randint(splits[10], (DEVICES * NBT, FAM), 0, 3 * NBT + 1), jax.random.fold_in(splits[10], 1), 0, 3 * NBT).astype(jnp.int32)
    ov_owner_keys = jax.random.split(jax.random.fold_in(splits[11], 1), OV_TOTAL // OV_DEV)
    ov_owner_turns = jax.random.permutation(jax.random.fold_in(splits[11], 3), OV_TOTAL // OV_DEV)
    ov_owner = jax.vmap(lambda own, number: deal_out(jax.random.fold_in(splits[11], 2), own, number, OV_DEV, N_LAT, 1, OCAP, 2))(ov_owner_keys, ov_owner_turns).reshape((OV_TOTAL, 1))
    ov_node = touch_ends(jax.random.randint(splits[12], (OV_TOTAL,), 0, NX * NY * NZ), jax.random.fold_in(splits[12], 1), 0, (NX * NY * NZ) - 1).astype(jnp.int32)
    ov_target = touch_ends(jax.random.randint(splits[13], (OV_TOTAL,), 0, P_OWN), jax.random.fold_in(splits[13], 1), 0, P_OWN - 1).astype(jnp.int32)
    ov_stiff = jnp.clip(jnp.exp(math.log(4.0) - 2.0794415 * jax.random.uniform(splits[14], (OV_TOTAL,), jnp.float32) ** block_scale(splits[14], (OV_TOTAL,), ((0, 32),), -0.2, 0.2)), 0.5, 4.0)
    return {"fem_disp": fem_disp, "fem_vel": fem_vel, "modulus": modulus, "inv_mass": inv_mass, "element_stiffness": element_stiffness, "pd_pos": pd_pos, "pd_disp": pd_disp, "pd_vel": pd_vel, "conv_state": conv_state, "conv_owner": conv_owner, "family": family, "ov_owner": ov_owner, "ov_node": ov_node, "ov_target": ov_target, "ov_stiff": ov_stiff}


time_step = 0.5
horizon_sq = 2.0
bond_gain = 8.0
highest = lax.Precision.HIGHEST


def element_forces(padded, stiffness):
    span_x = padded.shape[1] - 2
    span_y = padded.shape[2] - 2
    span_z = padded.shape[3] - 2
    corners = []
    for corner in range(8):
        shift_x = corner // 4
        shift_y = (corner // 2) % 2
        shift_z = corner % 2
        corners.append(padded[0:3, shift_x:shift_x + span_x + 1, shift_y:shift_y + span_y + 1, shift_z:shift_z + span_z + 1])
    stacked = jnp.concatenate(corners, axis=0)
    modulus = padded[3, 0:span_x + 1, 0:span_y + 1, 0:span_z + 1]
    element = jnp.einsum("ij,jxyz->ixyz", stiffness, stacked, precision=highest) * modulus[None]
    force = jnp.zeros((3, span_x, span_y, span_z), jnp.float32)
    for corner in range(8):
        shift_x = corner // 4
        shift_y = (corner // 2) % 2
        shift_z = corner % 2
        force = force + element[3 * corner:3 * corner + 3, 1 - shift_x:1 - shift_x + span_x, 1 - shift_y:1 - shift_y + span_y, 1 - shift_z:1 - shift_z + span_z]
    return force


def bond_forces(table, extended, family):
    count = table.shape[1] // BLOCK
    own_blocks = jnp.transpose(table.reshape(7, count, BLOCK), (1, 0, 2))
    ext_blocks = jnp.transpose(extended.reshape(7, -1, BLOCK), (1, 0, 2))
    scale = bond_gain / (BLOCK * family.shape[1])

    def one_block(inputs):
        mine, members = inputs
        others = jnp.take(ext_blocks, members, axis=0)
        dist = jnp.zeros((members.shape[0], BLOCK, BLOCK), jnp.float32)
        for comp in range(3):
            offset = others[:, comp][:, None, :] - mine[comp][None, :, None]
            dist = dist + offset * offset
        weight = jnp.exp(-dist / horizon_sq) * mine[6][None, :, None] * others[:, 6][:, None, :]
        pulled = jnp.einsum("fij,fcj->ci", weight, others[:, 3:6], precision=highest)
        total = jnp.sum(weight, axis=(0, 2))
        return scale * (pulled - mine[3:6] * total[None, :])

    forces = lax.map(one_block, (own_blocks, family))
    return jnp.transpose(forces, (1, 0, 2)).reshape(3, -1)


def reference(fem_disp, fem_vel, modulus, inv_mass, element_stiffness, pd_pos, pd_disp, pd_vel, conv_state, conv_owner, family, ov_owner, ov_node, ov_target, ov_stiff):
    stacked = jnp.concatenate([fem_disp, modulus[None]], axis=0)
    padded = jnp.pad(stacked, ((0, 0), (1, 1), (1, 1), (1, 1)))

    def fem_row(row):
        slab = lax.dynamic_slice(padded, (jnp.int32(0), row, jnp.int32(0), jnp.int32(0)), (4, 3, GY + 2, NZ + 2))
        return element_forces(slab, element_stiffness)[:, 0]

    internal = jnp.transpose(lax.map(fem_row, jnp.arange(GX, dtype=jnp.int32)), (1, 0, 2, 3))

    nodes = NX * NY * NZ

    def to_blocks(field):
        return jnp.transpose(field.reshape(3, N_DEPTH, NX, N_LAT, NY, NZ), (0, 1, 3, 2, 4, 5)).reshape(3, N_DEPTH, N_LAT, nodes)

    def from_blocks(field):
        return jnp.transpose(field.reshape(3, N_DEPTH, N_LAT, NX, NY, NZ), (0, 1, 3, 2, 4, 5)).reshape(3, GX, GY, NZ)

    grid_shape = (N_DEPTH, N_LAT, OV_DEV)
    depth_index = jnp.broadcast_to(jnp.arange(N_DEPTH, dtype=jnp.int32)[:, None, None], grid_shape)
    lat_index = jnp.broadcast_to(jnp.arange(N_LAT, dtype=jnp.int32)[None, :, None], grid_shape)
    ov_dest = ov_owner[:, 0].reshape(grid_shape)
    ov_where = ov_node.reshape(grid_shape)
    ov_point = ov_target.reshape(grid_shape)
    ov_gain = ov_stiff.reshape(grid_shape)
    fem_blocks = to_blocks(fem_disp)
    pd_blocks = pd_disp.reshape(3, N_DEPTH, N_LAT, P_OWN)
    fem_at = fem_blocks[:, depth_index, lat_index, ov_where]
    pd_at = pd_blocks[:, depth_index, ov_dest, ov_point]
    coupling = ov_gain[None] * (fem_at - pd_at)
    pd_couple = jnp.zeros_like(pd_blocks).at[:, depth_index, ov_dest, ov_point].add(coupling)
    fem_couple = from_blocks(jnp.zeros_like(fem_blocks).at[:, depth_index, lat_index, ov_where].add(-coupling))
    fem_vel_new = fem_vel + time_step * inv_mass[None] * (fem_couple - internal)

    conv_shape = (N_DEPTH, N_LAT, CONV_DEV)
    conv_dest = conv_owner[:, 0].reshape(conv_shape)
    match = (conv_dest[..., None] == jnp.arange(N_LAT, dtype=jnp.int32)).astype(jnp.int32)
    rank = jnp.sum((jnp.cumsum(match, axis=2) - 1) * match, axis=3)
    depth_conv = jnp.broadcast_to(jnp.arange(N_DEPTH, dtype=jnp.int32)[:, None, None], conv_shape)
    lat_conv = jnp.broadcast_to(jnp.arange(N_LAT, dtype=jnp.int32)[None, :, None], conv_shape)
    flat_slot = ((depth_conv * N_LAT + lat_conv) * N_LAT + conv_dest) * CAP + rank
    rows = jnp.concatenate([conv_state, jnp.ones((1, CONV_TOTAL), jnp.float32)], axis=0)
    buffer = jnp.zeros((N_DEPTH * N_LAT * N_LAT * CAP, 10), jnp.float32).at[flat_slot.reshape(-1)].set(jnp.transpose(rows))
    buffer = buffer.reshape(N_DEPTH, N_LAT, N_LAT, CAP, 10)
    tail = jnp.transpose(buffer, (0, 2, 4, 1, 3)).reshape(N_DEPTH, N_LAT, 10, TAIL)

    own = jnp.concatenate([pd_pos, pd_disp, jnp.ones((1, PD_OWN_TOTAL), jnp.float32)], axis=0)
    own = jnp.transpose(own.reshape(7, N_DEPTH, N_LAT, P_OWN), (1, 2, 0, 3))
    tail_rows = jnp.concatenate([tail[:, :, 0:6], tail[:, :, 9:10]], axis=2)
    table = jnp.concatenate([own, tail_rows], axis=3)
    bordered = jnp.pad(table, ((0, 0), (1, 1), (0, 0), (0, 0)))
    families = family.reshape(N_DEPTH * N_LAT, NBT, FAM)

    def device_bonds(index):
        depth_at = index // N_LAT
        lat_at = index % N_LAT
        near = lax.dynamic_slice(bordered, (depth_at, lat_at, jnp.int32(0), jnp.int32(0)), (1, 3, 7, P_DEV))[0]
        extended = jnp.transpose(near, (1, 0, 2)).reshape(7, 3 * P_DEV)
        extended = jnp.pad(extended, ((0, 0), (0, BLOCK)))
        members = lax.dynamic_index_in_dim(families, index, 0, keepdims=False)
        return bond_forces(near[1], extended, members)

    bonds = lax.map(device_bonds, jnp.arange(N_DEPTH * N_LAT, dtype=jnp.int32))
    bonds = bonds.reshape(N_DEPTH, N_LAT, 3, P_DEV)
    own_vel = jnp.transpose(pd_vel.reshape(3, N_DEPTH, N_LAT, P_OWN), (1, 2, 0, 3))
    own_new = own_vel + time_step * (bonds[..., :P_OWN] + jnp.transpose(pd_couple, (1, 2, 0, 3)))
    tail_new = tail[:, :, 6:9] + time_step * bonds[..., P_OWN:]
    pd_vel_new = jnp.transpose(jnp.concatenate([own_new, tail_new], axis=3), (2, 0, 1, 3)).reshape(3, PD_TOTAL)
    return fem_vel_new, pd_vel_new
```

```python
import functools
import math

import jax
import jax.numpy as jnp
from jax import lax
from jax.experimental import pallas as pl
from jax.experimental.pallas import tpu as pltpu
from jax.sharding import PartitionSpec as P

BLOCK = 128
CAP = 8
HALF = 0.5
GAIN = 8.0
LOG2E = math.log2(math.e)
F32 = jnp.float32
BF16 = jnp.bfloat16

VMEM = pl.BlockSpec(memory_space=pltpu.VMEM)
SMEM = pl.BlockSpec(memory_space=pltpu.SMEM)


def params():
    return pltpu.CompilerParams(vmem_limit_bytes=40 * 1024 * 1024)


def split3(value):
    high = value.astype(BF16)
    rest = value - high.astype(F32)
    mid = rest.astype(BF16)
    low = (rest - mid.astype(F32)).astype(BF16)
    return high, mid, low


def dot(a, b):
    return jnp.dot(a, b, preferred_element_type=F32)


def dot_nt(a, b):
    return lax.dot_general(a, b, (((1,), (1,)), ((), ())), preferred_element_type=F32)


def dot3(value, hot):
    high, mid, low = split3(value)
    return (dot(high, hot) + dot(mid, hot)) + dot(low, hot)


def dot3_nt(value, hot):
    high, mid, low = split3(value)
    return (dot_nt(high, hot) + dot_nt(mid, hot)) + dot_nt(low, hot)


def iota(shape, axis):
    return lax.broadcasted_iota(jnp.int32, shape, axis)


def one_hot(condition):
    return jnp.where(condition, 1.0, 0.0).astype(BF16)


def shift_of(size):
    assert size & (size - 1) == 0
    return size.bit_length() - 1


def point_rows(pos, disp):
    norm = (-0.5 * LOG2E) * (pos[0:1] * pos[0:1] + pos[1:2] * pos[1:2] + pos[2:3] * pos[2:3])
    return jnp.concatenate([disp, jnp.ones_like(norm), pos, norm], axis=0)


def slots_of(owner_ref):
    owner = owner_ref[...].astype(F32)
    rows = owner.shape[0]
    wide = jnp.broadcast_to(owner, (rows, rows))
    down, across = iota((rows, rows), 0), iota((rows, rows), 1)
    named = jnp.sum(jnp.where(down == across, wide, 0.0), axis=0, keepdims=True)
    earlier = jnp.where((wide == named) & (across < down), 1.0, 0.0)
    rank = jnp.sum(earlier, axis=1, keepdims=True)
    return owner * CAP + rank, named


def pack_kernel(
    peers,
    both_faces,
    info,
    fem_disp,
    modulus,
    pd_disp,
    conv_state,
    conv_owner,
    ov_owner,
    ov_node,
    ov_target,
    ov_stiff,
    chunk,
    faces,
    entries,
    rows_ref,
):
    nx, ny, nz = modulus.shape
    width = peers * CAP
    blocks = pd_disp.shape[1] // BLOCK
    count = ov_node.shape[1]
    for face, number in enumerate((0, nx - 1)):
        if both_faces:
            faces[face, 0:3] = fem_disp[:, number]
            faces[face, 3] = modulus[number]
    if not both_faces:
        upper = info[1] == 0
        faces[0, 0:3] = jnp.where(upper, fem_disp[:, nx - 1], fem_disp[:, 0])
        faces[0, 3] = jnp.where(upper, modulus[nx - 1], modulus[0])
    node = ov_node[...]
    hot_z = one_hot(iota((nz, count), 0) == (node & (nz - 1)))
    picked = dot3(fem_disp[...].reshape(3 * nx * ny, nz), hot_z)
    hot_xy = jnp.where(iota((nx * ny, count), 0) == (node >> shift_of(nz)), 1.0, 0.0)
    at_node = jnp.sum(picked.reshape(3, nx * ny, count) * hot_xy[None], axis=1)
    conv_slot, _ = slots_of(conv_owner)
    ov_slot, ov_named = slots_of(ov_owner)
    lane = iota((conv_slot.shape[0], width), 1).astype(F32)
    state = conv_state[...]
    points = point_rows(state[0:3], state[3:6])
    blank = jnp.zeros((5, state.shape[1]), F32)
    conv_rows = jnp.concatenate([points, state[6:9], blank], axis=0)
    stiff = ov_stiff[...]
    target = ov_target[...].astype(F32)
    ov_rows = jnp.concatenate([jnp.zeros((3, count), F32), at_node, stiff, target], axis=0)
    conv_out = dot3(conv_rows, one_hot(conv_slot == lane))
    ov_out = dot3(ov_rows, one_hot(ov_slot == lane))
    entries[...] = jnp.concatenate(
        [at_node, stiff, ov_named, target, node.astype(F32), jnp.zeros((1, count), F32)], axis=0
    )
    for block in range(blocks):
        for comp in range(3):
            rows_ref[comp * blocks + block : comp * blocks + block + 1] = pd_disp[
                comp : comp + 1, block * BLOCK : (block + 1) * BLOCK
            ]
    base = 3 * blocks
    for tile in range(width // BLOCK):
        part = slice(tile * BLOCK, (tile + 1) * BLOCK)
        rows_ref[base + 16 * tile : base + 16 * tile + 8] = conv_out[0:8, part]
        rows_ref[base + 16 * tile + 8 : base + 16 * tile + 16] = conv_out[8:16, part] + ov_out[:, part]
    value = rows_ref[...]
    for copy in range(chunk.shape[0]):
        chunk[copy] = value


def side_kernel(depth, info, fem_disp, modulus, pd_pos, pd_disp, low_x, high_x, pay_even, pay_odd):
    nx, ny, nz = modulus.shape
    blocks = pd_disp.shape[1] // BLOCK
    points = point_rows(pd_pos[...], pd_disp[...])
    for pair in range(blocks // 2):
        part = points[:, 2 * BLOCK * pair : 2 * BLOCK * (pair + 1)]
        pay_even[8 * pair : 8 * pair + 8] = part
        pay_odd[8 * pair : 8 * pair + 8] = part
    even = (info[0] & 1) == 0
    low_on = jnp.where(info[1] > 0, 1.0, 0.0)
    high_on = jnp.where(info[1] < depth - 1, 1.0, 0.0)
    base = 4 * blocks
    for pay, top in ((pay_even, even), (pay_odd, jnp.logical_not(even))):
        row = jnp.where(top, ny - 1, 0)
        for comp in range(4):
            at = base + comp
            pay[at : at + 1] = low_x[comp, pl.ds(row, 1)] * low_on
            for x in range(nx):
                at = base + 4 * (x + 1) + comp
                pay[at : at + 1] = fem_disp[comp, x, pl.ds(row, 1)] if comp < 3 else modulus[x, pl.ds(row, 1)]
            at = base + 4 * (nx + 1) + comp
            pay[at : at + 1] = high_x[comp, pl.ds(row, 1)] * high_on


def side_table(ref, block):
    return ref[8 * (block // 2) : 8 * (block // 2) + 8, BLOCK * (block % 2) : BLOCK * (block % 2 + 1)]


def own_features(points):
    row = iota(points.shape, 0)
    turned = pltpu.roll(points, 4, 0)
    value = jnp.where(row == 3, turned, jnp.where(row < 3, 0.0, jnp.where(row == 7, 1.0, LOG2E * points)))
    high, mid, low = (part.astype(F32) for part in split3(value))
    return jnp.concatenate([high, mid, high, mid, low, high], axis=0).astype(BF16)


def other_features(points):
    high, mid, low = (part.astype(F32) for part in split3(points))
    left = jnp.concatenate([high, high, mid, mid, high, low], axis=0)
    sums = jnp.concatenate([high, mid, low, jnp.zeros_like(low)], axis=0)
    return left.T.astype(BF16), sums.astype(BF16)


def pair_sums(left, sums, own):
    weight = jnp.exp2(dot(left, own))
    high = weight.astype(BF16)
    low = (weight - high.astype(F32)).astype(BF16)
    return dot(jnp.concatenate([sums, sums], axis=1), jnp.concatenate([high, low], axis=0))


def fold(total):
    return total[0:8] + total[8:16] + total[16:24]


def bond_kernel(tail_blocks, info, family, own, even_side, odd_side, sums_out, pairs, left_ref, sums_ref):
    blocks = sums_out.shape[0]
    table = blocks + tail_blocks
    members = family.shape[1]
    even = (info[0] & 1) == 0
    for block in range(blocks):
        first = side_table(even_side, block)
        second = side_table(odd_side, block)
        three = (jnp.where(even, second, first), side_table(own, block), jnp.where(even, first, second))
        for side, points in enumerate(three):
            left, sums = other_features(points)
            left_ref[side * blocks + block] = left
            sums_ref[side * blocks + block] = sums
    left_ref[3 * blocks] = jnp.zeros(left_ref.shape[1:], BF16)
    sums_ref[3 * blocks] = jnp.zeros(sums_ref.shape[1:], BF16)
    shift = shift_of(64)
    for block in range(blocks, table):
        for k in range(members):
            pairs[1 + (block - blocks) * members + k] = (block << shift) + family[block, k]

    def one(index, found):
        pair = index // 2
        points = own[pl.ds(pl.multiple_of(8 * index, 8), 8), :]
        for part in range(2):
            block = 2 * index + part
            mine = own_features(points[:, BLOCK * part : BLOCK * (part + 1)])
            total = jnp.zeros((32, BLOCK), F32)
            for k in range(members):
                member = family[block, k]
                side = jnp.where(member >= table, 1, 0) + jnp.where(member >= 2 * table, 1, 0)
                local = member - side * table
                outside = local >= blocks
                is_tail = outside & (member < 3 * table)
                pairs[1 + found] = (block << shift) + member
                found = found + jnp.where(is_tail, 1, 0)
                where = jnp.where(outside, 3 * blocks, side * blocks + local)
                total = total + pair_sums(left_ref[where], sums_ref[where], mine)
            sums_out[block] = fold(total)
        return found

    found = lax.fori_loop(0, blocks // 2, one, tail_blocks * members)
    for extra in range(4):
        pairs[1 + found + extra] = 3 * table
    pairs[0] = (found + 3) // 4


def stiffness_rows(stiffness):
    new, old = iota((32, 24), 0), iota((32, 24), 1)
    place = sum(
        jnp.where(old == k, (k // 3 // 2) * 8 + (k // 3 % 2) * 4 + k % 3, 0) for k in range(24)
    )
    hot = one_hot(new == place)
    parts = [dot_nt(dot(hot, part).astype(BF16), hot) for part in split3(stiffness)]
    high, mid, low = parts
    pieces = []
    for corner in range(4):
        part = slice(8 * corner, 8 * corner + 8)
        for piece in (high, high, mid, mid, high, low):
            pieces.append(piece[:, part])
    return jnp.concatenate(pieces, axis=1).astype(BF16)


def rock_kernel(
    depth,
    halo,
    info,
    fem_disp,
    fem_vel,
    modulus,
    inv_mass,
    stiffness,
    low_x,
    high_x,
    even_side,
    odd_side,
    out,
    nodes,
    first_ref,
    second_ref,
    force_ref,
):
    nx, ny, nz = modulus.shape
    wide = ny + 2
    even = (info[0] & 1) == 0
    low_on = jnp.where(info[1] > 0, 1.0, 0.0)
    high_on = jnp.where(info[1] < depth - 1, 1.0, 0.0)
    lane_end = iota((8, nz), 1) == nz - 1

    def ahead(value):
        return jnp.where(lane_end[0 : value.shape[0]], 0.0, pltpu.roll(value, nz - 1, 1))

    halves = [slice(h * BLOCK, (h + 1) * BLOCK) for h in range(nz // BLOCK)]
    for x in range(nx + 2):
        for comp in range(4):
            if x == 0:
                value = low_x[comp] * low_on
            elif x == nx + 1:
                value = high_x[comp] * high_on
            else:
                value = fem_disp[comp, x - 1] if comp < 3 else modulus[x - 1]
            at = (x * wide + 1) * 8 + comp
            shifted = ahead(value)
            for half, part in enumerate(halves):
                nodes[half, pl.ds(at, ny, stride=8), :] = value[:, part]
                nodes[half, pl.ds(at + 4, ny, stride=8), :] = shifted[:, part]
        for y, from_even in ((0, jnp.logical_not(even)), (ny + 1, even)):
            rows = slice(halo + 4 * x, halo + 4 * x + 4)
            value = jnp.where(from_even, even_side[rows], odd_side[rows])
            at = (x * wide + y) * 8
            shifted = ahead(value)
            for half, part in enumerate(halves):
                nodes[half, at : at + 4, :] = value[:, part]
                nodes[half, at + 4 : at + 8, :] = shifted[:, part]

    row8 = iota((8, nz), 0)
    keep = (row8 != 3) & (row8 != 7)

    def node_row(x, y):
        at = (x * wide + y) * 8
        return jnp.concatenate([nodes[h, at : at + 8, :] for h in range(len(halves))], axis=1)

    for x in range(nx + 2):
        for y in range(wide):
            value = jnp.where(keep, node_row(x, y), 0.0)
            high, mid, low = (part.astype(F32) for part in split3(value))
            first_ref[x * wide + y] = jnp.concatenate([high, mid], axis=0).astype(BF16)
            second_ref[x * wide + y] = jnp.concatenate([low, high], axis=0).astype(BF16)
    left = stiffness_rows(stiffness[...])

    def element(x, y):
        pieces = []
        for a in range(2):
            for b in range(2):
                at = (x + a) * wide + y + b
                pieces += [first_ref[at], first_ref[at], second_ref[at]]
        force = dot(left, jnp.concatenate(pieces, axis=0))
        return force * node_row(x, y)[3:4]

    row_keep = iota((8, nz), 1) != 0
    before = None
    for x in range(nx + 1):
        line = [element(x, y) for y in range(ny + 1)]
        if x > 0:
            for y in range(1, ny + 1):
                total = line[y][0:8] + line[y - 1][8:16] + before[y][16:24] + before[y - 1][24:32]
                turned = pltpu.roll(pltpu.roll(total, 4, 0), 1, 1)
                total = total + jnp.where(row_keep, turned, 0.0)
                at = ((x - 1) * ny + y - 1) * 8
                for half, part in enumerate(halves):
                    force_ref[half, at : at + 8, :] = total[:, part]
        before = line
    for x in range(nx):
        for comp in range(3):
            force = jnp.concatenate(
                [force_ref[h, pl.ds(x * ny * 8 + comp, ny, stride=8), :] for h in range(len(halves))], axis=1
            )
            out[comp, x] = fem_vel[comp, x] - HALF * inv_mass[x] * force


def final_kernel(
    peers,
    members,
    info,
    pairs,
    mine_in,
    mate_in,
    entries,
    rock,
    inv_mass,
    sums_in,
    own,
    even_side,
    odd_side,
    pd_vel,
    fem_out,
    pd_out,
    table_ref,
    sums_ref,
):
    nx, ny, nz = inv_mass.shape
    width = peers * CAP
    tail_blocks = width // BLOCK
    blocks = sums_in.shape[0]
    table = blocks + tail_blocks
    base = 3 * blocks
    place = info[0]
    core = place & 1
    even = core == 0
    for block in range(blocks):
        first = side_table(even_side, block)
        second = side_table(odd_side, block)
        table_ref[block] = jnp.where(even, second, first)
        table_ref[table + block] = side_table(own, block)
        table_ref[2 * table + block] = jnp.where(even, first, second)
        sums_ref[block] = sums_in[block]
    table_ref[3 * table] = jnp.zeros((8, BLOCK), F32)
    for block in range(blocks, table):
        sums_ref[block] = jnp.zeros((8, BLOCK), F32)

    def slot_rows(ref, k):
        tiles = [ref[k, base + 16 * tile : base + 16 * tile + 16, :] for tile in range(tail_blocks)]
        return tiles[0] if tail_blocks == 1 else jnp.concatenate(tiles, axis=1)

    lane = iota((16, width), 1)
    back = lax.rem(width - CAP * (place - 1) + width, width)
    tails = [jnp.zeros((16, width), F32) for _ in range(3)]
    for ref, odd in ((mine_in, core), (mate_in, 1 - core)):
        gathered = [jnp.zeros((16, width), F32) for _ in range(3)]
        for k in range(peers // 2):
            turned = pltpu.roll(slot_rows(ref, k), back, 1)
            for side in range(3):
                window = jnp.where((lane >= CAP * side) & (lane < CAP * side + CAP), turned, 0.0)
                amount = (2 * CAP * k - CAP * side) % width
                gathered[side] = gathered[side] + (pltpu.roll(window, amount, 1) if amount else window)
        for side in range(3):
            tails[side] = tails[side] + pltpu.roll(gathered[side], CAP * odd, 1)
    on = (jnp.where(place > 0, 1.0, 0.0), 1.0, jnp.where(place < peers - 1, 1.0, 0.0))
    for side in range(3):
        for tile in range(tail_blocks):
            part = tails[side][0:8, tile * BLOCK : (tile + 1) * BLOCK]
            table_ref[side * table + blocks + tile] = part * on[side]
    tail_rows = tails[1]

    shift = shift_of(64)

    def some(index, carry):
        results = []
        for lane_of in range(4):
            code = pairs[1 + 4 * index + lane_of]
            block = code >> shift
            left, sums = other_features(table_ref[code & 63])
            results.append((block, fold(pair_sums(left, sums, own_features(table_ref[table + block])))))
        for block, total in results:
            sums_ref[block] = sums_ref[block] + total
        return carry

    lax.fori_loop(0, pairs[0], some, 0)

    stiff = tail_rows[14:15]
    target = tail_rows[15:16].astype(jnp.int32)
    hot_lane = one_hot(iota((BLOCK, width), 0) == (target & (BLOCK - 1)))
    target_block = target >> shift_of(BLOCK)
    tables = jnp.concatenate([table_ref[table + block] for block in range(blocks)], axis=0)
    looked = dot3(tables, hot_lane)
    found = jnp.zeros((8, width), F32)
    for block in range(blocks):
        found = found + jnp.where(target_block == block, looked[8 * block : 8 * block + 8], 0.0)
    coupling = stiff * (tail_rows[11:14] - found[0:3])
    coupling = jnp.concatenate([coupling, jnp.zeros((5, width), F32)], axis=0)
    spread = jnp.concatenate([jnp.where(target_block == block, coupling, 0.0) for block in range(blocks)], axis=0)
    couple = dot3_nt(spread, hot_lane)

    scale = GAIN / (BLOCK * members)
    for block in range(table):
        total = sums_ref[block]
        points = table_ref[table + block]
        part = slice(block * BLOCK, (block + 1) * BLOCK)
        force = scale * points[3:4] * (total[0:3] - points[0:3] * total[3:4])
        if block < blocks:
            pd_out[:, part] = pd_vel[:, part] + HALF * (force + couple[8 * block : 8 * block + 3])
        else:
            tile = block - blocks
            pd_out[:, part] = tail_rows[8:11, tile * BLOCK : (tile + 1) * BLOCK] + HALF * force

    entry = entries[...]
    count = entry.shape[1]
    owner = entry[4:5].astype(jnp.int32)
    goal = entry[5:6].astype(jnp.int32)
    node = entry[6:7].astype(jnp.int32)
    pick = one_hot(iota((BLOCK, count), 0) == (goal & (BLOCK - 1)))
    goal_row = (owner >> 1) * blocks + (goal >> shift_of(BLOCK))
    from_mine = (owner & 1) == core
    rows = peers // 2 * blocks
    hit = iota((rows, count), 0) == goal_row
    values = []
    for comp in range(3):
        part = slice(comp * blocks, (comp + 1) * blocks)
        value = jnp.zeros((1, count), F32)
        for ref, wanted in ((mine_in, from_mine), (mate_in, jnp.logical_not(from_mine))):
            got = dot3(ref[:, part, :].reshape(rows, BLOCK), pick)
            value = value + jnp.sum(jnp.where(hit & wanted, got, 0.0), axis=0, keepdims=True)
        values.append(value)
    z_hot = one_hot(iota((nz, count), 0) == (node & (nz - 1)))
    xy_hit = iota((nx * ny, count), 0) == (node >> shift_of(nz))
    spread = jnp.concatenate(
        [jnp.where(xy_hit, entry[3:4] * (entry[c : c + 1] - values[c]), 0.0) for c in range(3)], axis=0
    )
    pull = dot3_nt(spread, z_hot).reshape(3, nx, ny, nz)
    fem_out[...] = rock[...] - HALF * inv_mass[...][None] * pull


def call(kernel, outs, specs, scratch, flops, nbytes, args, name, out_specs=None):
    return pl.pallas_call(
        kernel,
        out_shape=outs,
        in_specs=specs,
        out_specs=out_specs or jax.tree.map(lambda _: VMEM, outs),
        scratch_shapes=scratch,
        compiler_params=params(),
        cost_estimate=pl.CostEstimate(flops=flops, bytes_accessed=nbytes, transcendentals=0),
        name=name,
    )(*args)


def shards(
    fem_disp,
    fem_vel,
    modulus,
    inv_mass,
    element_stiffness,
    pd_pos,
    pd_disp,
    pd_vel,
    conv_state,
    conv_owner,
    family,
    ov_owner,
    ov_node,
    ov_target,
    ov_stiff,
):
    peers = lax.axis_size("lat")
    depth = lax.axis_size("depth")
    nx, ny, nz = modulus.shape
    blocks = pd_pos.shape[1] // BLOCK
    tail_blocks = peers * CAP // BLOCK
    table = blocks + tail_blocks
    members = family.shape[1]
    count = ov_node.shape[0]
    chips = peers // 2
    chunk_rows = 3 * blocks + 16 * tail_blocks
    shaped = jax.ShapeDtypeStruct
    info = jnp.stack([lax.axis_index("lat"), lax.axis_index("depth")]).astype(jnp.int32)

    both_faces = depth > 2
    chunk, faces, entries = call(
        functools.partial(pack_kernel, peers, both_faces),
        (
            shaped((chips, chunk_rows, BLOCK), F32),
            shaped((2 if both_faces else 1, 4, ny, nz), F32),
            shaped((8, count), F32),
        ),
        [SMEM] + [VMEM] * 9,
        [pltpu.VMEM((chunk_rows, BLOCK), F32)],
        4_000_000,
        400_000,
        (
            info,
            fem_disp,
            modulus,
            pd_disp,
            conv_state,
            conv_owner,
            ov_owner,
            ov_node.reshape(1, -1),
            ov_target.reshape(1, -1),
            ov_stiff.reshape(1, -1),
        ),
        "pack",
    )
    if both_faces:
        low_x = lax.ppermute(faces[1], "depth", [(i, i + 1) for i in range(depth - 1)])
        high_x = lax.ppermute(faces[0], "depth", [(i + 1, i) for i in range(depth - 1)])
    else:
        low_x = high_x = lax.ppermute(faces[0], "depth", [(0, 1), (1, 0)])
    groups = [[side + 2 * k for k in range(chips)] for side in range(2)]
    mine = lax.all_to_all(chunk, "lat", split_axis=0, concat_axis=0, tiled=True, axis_index_groups=groups)

    halo = 4 * blocks
    pay_rows = halo + 4 * (nx + 2)
    pay_even, pay_odd = call(
        functools.partial(side_kernel, depth),
        (shaped((pay_rows, nz), F32),) * 2,
        [SMEM] + [VMEM] * 6,
        [],
        1_000_000,
        400_000,
        (info, fem_disp, modulus, pd_pos, pd_disp, low_x, high_x),
        "side",
    )
    swap = [(i, i ^ 1) for i in range(peers)]
    cross = [(i, i + 1) for i in range(1, peers - 1, 2)] + [(i + 1, i) for i in range(1, peers - 1, 2)]
    odd_side = lax.ppermute(pay_odd, "lat", cross)
    even_side = lax.ppermute(pay_even, "lat", swap)

    sums, pairs = call(
        functools.partial(bond_kernel, tail_blocks),
        (shaped((blocks, 8, BLOCK), F32), shaped((table * members + 8,), jnp.int32)),
        [SMEM, SMEM] + [VMEM] * 3,
        [pltpu.VMEM((3 * blocks + 1, BLOCK, 48), BF16), pltpu.VMEM((3 * blocks + 1, 32, BLOCK), BF16)],
        200_000_000,
        10_000_000,
        (info, family, pay_even, even_side, odd_side),
        "bond",
        out_specs=(VMEM, SMEM),
    )
    mine, sums = lax.optimization_barrier((mine, sums))
    mate = lax.ppermute(mine, "lat", swap)
    rock = call(
        functools.partial(rock_kernel, depth, halo),
        shaped(fem_vel.shape, F32),
        [SMEM] + [VMEM] * 9,
        [
            pltpu.VMEM((nz // BLOCK, (nx + 2) * (ny + 2) * 8, BLOCK), F32),
            pltpu.VMEM(((nx + 2) * (ny + 2), 16, nz), BF16),
            pltpu.VMEM(((nx + 2) * (ny + 2), 16, nz), BF16),
            pltpu.VMEM((nz // BLOCK, nx * ny * 8, BLOCK), F32),
        ],
        100_000_000,
        5_000_000,
        (info, fem_disp, fem_vel, modulus, inv_mass, element_stiffness, low_x, high_x, even_side, odd_side),
        "rock",
    )
    return call(
        functools.partial(final_kernel, peers, members),
        (shaped(fem_vel.shape, F32), shaped((3, table * BLOCK), F32)),
        [SMEM, SMEM] + [VMEM] * 10,
        [pltpu.VMEM((3 * table + 1, 8, BLOCK), F32), pltpu.VMEM((table, 8, BLOCK), F32)],
        20_000_000,
        2_000_000,
        (info, pairs, mine, mate, entries, rock, inv_mass, sums, pay_even, even_side, odd_side, pd_vel),
        "final",
    )


def solution(mesh):
    lat = P(None, ("depth", "lat"))
    rows = P(("depth", "lat"), None)
    flat = P(("depth", "lat"))
    nodes = P(None, "depth", "lat", None)
    grid = P("depth", "lat", None)
    return jax.shard_map(
        shards,
        mesh=mesh,
        in_specs=(nodes, nodes, grid, grid, P(), lat, lat, lat, lat, rows, rows, rows, flat, flat, flat),
        out_specs=(nodes, lat),
        check_vma=False,
    )
```

```python
import functools
import math

import jax
import jax.numpy as jnp
from jax import lax
from jax.experimental import pallas as pl
from jax.experimental.pallas import tpu as pltpu
from jax.sharding import PartitionSpec as P

BLOCK = 128
CAP = 8
HALF = 0.5
GAIN = 8.0
LOG2E = math.log2(math.e)
F32 = jnp.float32
BF16 = jnp.bfloat16
LAG = 8
BATCH = 8
PAIR_SHIFT = 6
SIDE_VMEM = 63

VMEM = pl.BlockSpec(memory_space=pltpu.VMEM)
SMEM = pl.BlockSpec(memory_space=pltpu.SMEM)
FAR = pl.BlockSpec(memory_space=pltpu.HBM)
ANY = pl.BlockSpec(memory_space=pl.ANY)


def params(mebibytes):
    return pltpu.CompilerParams(vmem_limit_bytes=int(mebibytes * 1024 * 1024))


def split3(value):
    high = value.astype(BF16)
    rest = value - high.astype(F32)
    mid = rest.astype(BF16)
    low = (rest - mid.astype(F32)).astype(BF16)
    return high, mid, low


def dot(a, b):
    return jnp.dot(a, b, preferred_element_type=F32)


def dot_nt(a, b):
    return lax.dot_general(a, b, (((1,), (1,)), ((), ())), preferred_element_type=F32)


def dot3(value, hot):
    high, mid, low = split3(value)
    return (dot(high, hot) + dot(mid, hot)) + dot(low, hot)


def dot3_nt(value, hot):
    high, mid, low = split3(value)
    return (dot_nt(high, hot) + dot_nt(mid, hot)) + dot_nt(low, hot)


def iota(shape, axis):
    return lax.broadcasted_iota(jnp.int32, shape, axis)


def one_hot(condition):
    return jnp.where(condition, 1.0, 0.0).astype(BF16)


def shift_of(size):
    assert size & (size - 1) == 0
    return size.bit_length() - 1


def point_rows(pos, disp):
    norm = (-0.5 * LOG2E) * (pos[0:1] * pos[0:1] + pos[1:2] * pos[1:2] + pos[2:3] * pos[2:3])
    return jnp.concatenate([disp, jnp.ones_like(norm), pos, norm], axis=0)


def slots_of(owner_ref):
    named = owner_ref[...].astype(F32)
    rows = named.shape[1]
    wide = jnp.broadcast_to(named, (rows, rows))
    down, across = iota((rows, rows), 0), iota((rows, rows), 1)
    owner = jnp.sum(jnp.where(down == across, wide, 0.0), axis=1, keepdims=True)
    earlier = jnp.where((wide == owner) & (across < down), 1.0, 0.0)
    rank = jnp.sum(earlier, axis=1, keepdims=True)
    return owner * CAP + rank, named


def fetch(sources, places, sems):
    copies = [pltpu.make_async_copy(f, t, sems.at[i]) for i, (f, t) in enumerate(zip(sources, places))]
    for copy in copies:
        copy.start()
    for copy in copies:
        copy.wait()


def pack_kernel(
    peers,
    fem_disp,
    pd_disp,
    conv_state,
    conv_owner,
    ov_owner,
    ov_node,
    ov_target,
    ov_stiff,
    chunk,
    entries,
    rows_ref,
):
    _, nx, ny, nz = fem_disp.shape
    width = peers * CAP
    blocks = pd_disp.shape[1] // BLOCK
    count = ov_node.shape[1]
    node = ov_node[...]
    hot_z = one_hot(iota((nz, count), 0) == (node & (nz - 1)))
    picked = dot3(fem_disp[...].reshape(3 * nx * ny, nz), hot_z)
    hot_xy = jnp.where(iota((nx * ny, count), 0) == (node >> shift_of(nz)), 1.0, 0.0)
    at_node = jnp.sum(picked.reshape(3, nx * ny, count) * hot_xy[None], axis=1)
    conv_slot, _ = slots_of(conv_owner)
    ov_slot, ov_named = slots_of(ov_owner)
    lane = iota((conv_slot.shape[0], width), 1).astype(F32)
    state = conv_state[...]
    points = point_rows(state[0:3], state[3:6])
    blank = jnp.zeros((5, state.shape[1]), F32)
    conv_rows = jnp.concatenate([points, state[6:9], blank], axis=0)
    stiff = ov_stiff[...]
    target = ov_target[...].astype(F32)
    ov_rows = jnp.concatenate([jnp.zeros((3, count), F32), at_node, stiff, target], axis=0)
    conv_out = dot3(conv_rows, one_hot(conv_slot == lane))
    ov_out = dot3(ov_rows, one_hot(ov_slot == lane))
    entries[...] = jnp.concatenate(
        [at_node, stiff, ov_named, target, node.astype(F32), jnp.zeros((1, count), F32)], axis=0
    )
    for block in range(blocks):
        for comp in range(3):
            rows_ref[comp * blocks + block : comp * blocks + block + 1] = pd_disp[
                comp : comp + 1, block * BLOCK : (block + 1) * BLOCK
            ]
    base = 3 * blocks
    for tile in range(width // BLOCK):
        part = slice(tile * BLOCK, (tile + 1) * BLOCK)
        rows_ref[base + 16 * tile : base + 16 * tile + 8] = conv_out[0:8, part]
        rows_ref[base + 16 * tile + 8 : base + 16 * tile + 16] = conv_out[8:16, part] + ov_out[:, part]
    value = rows_ref[...]
    for copy in range(chunk.shape[0]):
        chunk[copy] = value


def side_kernel(
    fem_disp_in, modulus_in, pd_pos_in, pd_disp_in, pay_even, pay_odd, fem_disp, modulus, pd_pos, pd_disp, sems
):
    fetch((fem_disp_in, modulus_in, pd_pos_in, pd_disp_in), (fem_disp, modulus, pd_pos, pd_disp), sems)
    nx, ny, nz = modulus.shape
    blocks = pd_disp.shape[1] // BLOCK
    points = point_rows(pd_pos[...], pd_disp[...])
    for pair in range(blocks // 2):
        part = points[:, 2 * BLOCK * pair : 2 * BLOCK * (pair + 1)]
        pay_even[8 * pair : 8 * pair + 8] = part
        pay_odd[8 * pair : 8 * pair + 8] = part
    even = (lax.axis_index("lat") & 1) == 0
    for pay, top in ((pay_even, even), (pay_odd, jnp.logical_not(even))):
        row = jnp.where(top, ny - 1, 0)
        for x in range(nx):
            for comp in range(4):
                at = halo_row(4 * x + comp)
                pay[at : at + 1] = fem_disp[comp, x, pl.ds(row, 1)] if comp < 3 else modulus[x, pl.ds(row, 1)]


def halo_row(number):
    return 8 * (number // 2) + 3 + 4 * (number % 2)


def halo_rows(ref, x):
    return jnp.concatenate([ref[halo_row(4 * x + c) : halo_row(4 * x + c) + 1] for c in range(4)], axis=0)


def face_kernel(both_faces, info, fem_disp, modulus, even_side, odd_side, faces):
    nx, ny, nz = modulus.shape
    even = (info[0] & 1) == 0

    def rows_at(number):
        upper = halo_rows(even_side, number), halo_rows(odd_side, number)
        return jnp.where(even, upper[1], upper[0]), jnp.where(even, upper[0], upper[1])

    def put(face, chosen, low, high):
        for comp in range(4):
            faces[face, comp, 0:ny] = chosen(comp)
            faces[face, comp, ny : ny + 1] = low[comp : comp + 1]
            faces[face, comp, ny + 1 : ny + 2] = high[comp : comp + 1]

    def layer(number):
        return lambda comp: fem_disp[comp, number] if comp < 3 else modulus[number]

    if both_faces:
        for face, number in ((0, 0), (1, nx - 1)):
            put(face, layer(number), *rows_at(number))
    else:
        upper = info[1] == 0
        first, second = rows_at(nx - 1), rows_at(0)
        put(
            0,
            lambda comp: jnp.where(upper, layer(nx - 1)(comp), layer(0)(comp)),
            jnp.where(upper, first[0], second[0]),
            jnp.where(upper, first[1], second[1]),
        )


def side_table(ref, block):
    rows = ref[8 * (block // 2) : 8 * (block // 2) + 8, BLOCK * (block % 2) : BLOCK * (block % 2 + 1)]
    row = iota(rows.shape, 0)
    squares = jnp.where((row >= 4) & (row < 7), rows * rows, 0.0)
    norm = (-0.5 * LOG2E) * jnp.sum(squares, axis=0, keepdims=True)
    return jnp.where(row == 3, 1.0, jnp.where(row == 7, norm, rows))


def own_features(points):
    row = iota(points.shape, 0)
    turned = pltpu.roll(points, 4, 0)
    value = jnp.where(row == 3, turned, jnp.where(row < 3, 0.0, jnp.where(row == 7, 1.0, LOG2E * points)))
    high, mid, low = (part.astype(F32) for part in split3(value))
    return jnp.concatenate([high, mid, high, mid, low, high], axis=0).astype(BF16)


def other_features(points):
    high, mid, low = (part.astype(F32) for part in split3(points))
    left = jnp.concatenate([high, high, mid, mid, high, low], axis=0)
    sums = jnp.concatenate([high, mid, low, jnp.zeros_like(low)], axis=0)
    return left.astype(BF16).T, sums.astype(BF16)


def pair_weights(left, own):
    weight = jnp.exp2(dot(left, own))
    high = weight.astype(BF16)
    low = (weight - high.astype(F32)).astype(BF16)
    return jnp.concatenate([high, low], axis=0)


def weighted(sums, weights):
    return dot(jnp.concatenate([sums, sums], axis=1), weights)


def fold(total):
    return total[0:8] + total[8:16] + total[16:24]


def neighbours(peers, place, first, second):
    even = (place & 1) == 0
    before = jnp.where(place > 0, jnp.where(even, second, first), 0.0)
    return before, jnp.where(place < peers - 1, jnp.where(even, first, second), 0.0)


def bond_kernel(peers, tail_blocks, members, info, family, own, even_side, odd_side, after, sums_out, pairs, left_ref, sums_ref):
    blocks = sums_out.shape[0]
    table = blocks + tail_blocks
    for block in range(blocks):
        first = side_table(even_side, block)
        second = side_table(odd_side, block)
        before, after = neighbours(peers, info[0], first, second)
        three = (before, side_table(own, block), after)
        for side, points in enumerate(three):
            left, sums = other_features(points)
            left_ref[side * blocks + block] = left
            sums_ref[side * blocks + block] = sums
    left_ref[3 * blocks] = jnp.zeros(left_ref.shape[1:], BF16)
    sums_ref[3 * blocks] = jnp.zeros(sums_ref.shape[1:], BF16)
    found = jnp.int32(0)
    mine, totals, places, weights = {}, {}, {}, {}
    units = blocks * members
    for unit in range(units + LAG):
        if unit < units:
            block, k = divmod(unit, members)
            if k == 0:
                mine[block] = own_features(side_table(own, block))
            member = family[k, block]
            side = jnp.where(member >= table, 1, 0) + jnp.where(member >= 2 * table, 1, 0)
            local = member - side * table
            outside = local >= blocks
            pairs[1 + found] = (block << PAIR_SHIFT) + member
            found = found + jnp.where(outside & (member < 3 * table), 1, 0)
            places[unit] = jnp.where(outside, 3 * blocks, side * blocks + local)
            weights[unit] = pair_weights(left_ref[places[unit]], mine[block])
        if unit >= LAG:
            done = unit - LAG
            block, k = divmod(done, members)
            total = weighted(sums_ref[places[done]], weights.pop(done))
            totals[block] = total if k == 0 else totals[block] + total
            if k == members - 1:
                sums_out[block] = fold(totals.pop(block))
    for extra in range(BATCH):
        pairs[1 + found + extra] = 3 * table
    pairs[0] = (found + BATCH - 1) // BATCH


def stiffness_rows(stiffness):
    new, old = iota((32, 24), 0), iota((32, 24), 1)
    place = sum(
        jnp.where(old == k, (k // 3 // 2) * 8 + (k // 3 % 2) * 4 + k % 3, 0) for k in range(24)
    )
    hot = one_hot(new == place)
    parts = [dot_nt(dot(hot, part).astype(BF16), hot) for part in split3(stiffness)]
    high, mid, low = parts
    pieces = []
    for corner in range(4):
        part = slice(8 * corner, 8 * corner + 8)
        for piece in (high, high, mid, mid, high, low):
            pieces.append(piece[:, part])
    return jnp.concatenate(pieces, axis=1).astype(BF16)


def ahead(value):
    last = value.shape[1] - 1
    return jnp.where(iota(value.shape, 1) == last, 0.0, pltpu.roll(value, last, 1))


def node_parts(node):
    row = iota(node.shape, 0)
    value = jnp.where((row != 3) & (row != 7), node, 0.0)
    high, mid, low = (part.astype(F32) for part in split3(value))
    first = jnp.concatenate([high, mid], axis=0).astype(BF16)
    return first, jnp.concatenate([low, high], axis=0).astype(BF16)


def gathered_force(total):
    turned = pltpu.roll(pltpu.roll(total, 4, 0), 1, 1)
    return total + jnp.where(iota(total.shape, 1) != 0, turned, 0.0)


def rock_kernel(
    depth,
    info,
    fem_disp,
    fem_vel,
    modulus,
    inv_mass,
    stiffness,
    low_x,
    high_x,
    after,
    out,
    edge_nodes,
    left_out,
    nodes,
    first_ref,
    second_ref,
    force_ref,
):
    nx, ny, nz = modulus.shape
    low_on = jnp.where(info[1] > 0, 1.0, 0.0)
    high_on = jnp.where(info[1] < depth - 1, 1.0, 0.0)
    halves = [slice(h * BLOCK, (h + 1) * BLOCK) for h in range(nz // BLOCK)]
    left = stiffness_rows(stiffness[...])
    left_out[...] = left
    for x in range(nx + 2):
        for comp in range(4):
            if x == 0:
                value = low_x[comp, 0:ny] * low_on
            elif x == nx + 1:
                value = high_x[comp, 0:ny] * high_on
            else:
                value = fem_disp[comp, x - 1] if comp < 3 else modulus[x - 1]
            at = x * ny * 8 + comp
            shifted = ahead(value)
            for half, part in enumerate(halves):
                nodes[half, pl.ds(at, ny, stride=8), :] = value[:, part]
                nodes[half, pl.ds(at + 4, ny, stride=8), :] = shifted[:, part]

    def node_row(x, y):
        at = (x * ny + y) * 8
        return jnp.concatenate([nodes[h, at : at + 8, :] for h in range(len(halves))], axis=1)

    for x in range(nx + 2):
        for y in range(ny):
            node = node_row(x, y)
            if y in (0, ny - 1):
                edge_nodes[0 if y == 0 else 1, x] = node
            first, second = node_parts(node)
            first_ref[x * ny + y] = first
            second_ref[x * ny + y] = second

    def element(x, y):
        pieces = []
        for a in range(2):
            for b in range(2):
                at = (x + a) * ny + y + b
                pieces += [first_ref[at], first_ref[at], second_ref[at]]
        return dot(left, jnp.concatenate(pieces, axis=0)) * node_row(x, y)[3:4]

    before = None
    for x in range(nx + 1):
        line = [element(x, y) for y in range(ny - 1)]
        if x > 0:
            for y in range(ny):
                terms = []
                if y < ny - 1:
                    terms += [line[y][0:8], before[y][16:24]]
                if y > 0:
                    terms += [line[y - 1][8:16], before[y - 1][24:32]]
                total = gathered_force(sum(terms[1:], terms[0]))
                at = ((x - 1) * ny + y) * 8
                for half, part in enumerate(halves):
                    force_ref[half, at : at + 8, :] = total[:, part]
        before = line
    for x in range(nx):
        for comp in range(3):
            force = jnp.concatenate(
                [force_ref[h, pl.ds(x * ny * 8 + comp, ny, stride=8), :] for h in range(len(halves))], axis=1
            )
            out[comp, x] = fem_vel[comp, x] - HALF * inv_mass[x] * force


def received(ref, peers, blocks, place, odd, wanted, row, pick):
    width = peers * CAP
    base = 3 * blocks

    def slot_rows(k):
        tiles = [ref[k, base + 16 * t : base + 16 * t + 16, :] for t in range(width // BLOCK)]
        return tiles[0] if len(tiles) == 1 else jnp.concatenate(tiles, axis=1)

    lane = iota((16, width), 1)
    back = lax.rem(width - CAP * (place - 1) + width, width)
    gathered = [jnp.zeros((16, width), F32) for _ in range(3)]
    for k in range(peers // 2):
        turned = pltpu.roll(slot_rows(k), back, 1)
        for side in range(3):
            window = jnp.where((lane >= CAP * side) & (lane < CAP * side + CAP), turned, 0.0)
            amount = (2 * CAP * k - CAP * side) % width
            gathered[side] = gathered[side] + (pltpu.roll(window, amount, 1) if amount else window)
    tails = [pltpu.roll(part, CAP * odd, 1) for part in gathered]
    rows = peers // 2 * blocks
    hit = (iota((rows, pick.shape[1]), 0) == row) & wanted
    values = []
    for comp in range(3):
        got = dot3(ref[:, comp * blocks : (comp + 1) * blocks, :].reshape(rows, BLOCK), pick)
        values.append(jnp.sum(jnp.where(hit, got, 0.0), axis=0, keepdims=True))
    return tails, values


def entry_places(entry, blocks):
    owner = entry[4:5].astype(jnp.int32)
    goal = entry[5:6].astype(jnp.int32)
    pick = one_hot(iota((BLOCK, entry.shape[1]), 0) == (goal & (BLOCK - 1)))
    return owner & 1, (owner >> 1) * blocks + (goal >> shift_of(BLOCK)), pick


def edge_kernel(
    peers,
    depth,
    blocks,
    info,
    mine_in,
    entries,
    rock,
    inv_mass,
    edge_nodes,
    left_in,
    low_x,
    high_x,
    even_side,
    odd_side,
    out,
    tails_out,
    values_out,
):
    nx, ny, nz = inv_mass.shape
    place = info[0]
    core = place & 1
    even = core == 0
    entry = entries[...]
    odd_owner, row, pick = entry_places(entry, blocks)
    tails, values = received(mine_in, peers, blocks, place, core, odd_owner == core, row, pick)
    for side in range(3):
        tails_out[side] = tails[side]
    values_out[...] = jnp.concatenate(values + [jnp.zeros((5, entry.shape[1]), F32)], axis=0)

    left = left_in[...]
    low_on = jnp.where(info[1] > 0, 1.0, 0.0)
    high_on = jnp.where(info[1] < depth - 1, 1.0, 0.0)
    for edge, from_even, node_y in ((0, jnp.logical_not(even), 0), (1, even, ny - 1)):
        inner, outer, lower = [], [], []
        for x in range(nx + 2):
            if x == 0:
                value = low_x[:, ny + edge] * low_on
            elif x == nx + 1:
                value = high_x[:, ny + edge] * high_on
            else:
                value = jnp.where(from_even, halo_rows(even_side, x - 1), halo_rows(odd_side, x - 1))
            other = jnp.concatenate([value, ahead(value)], axis=0)
            node = edge_nodes[edge, x]
            lower.append((other if edge == 0 else node)[3:4])
            inner.append(node_parts(node))
            outer.append(node_parts(other))
        forces = []
        for x in range(nx + 1):
            pieces = []
            for a in range(2):
                for b in range(2):
                    first, second = (outer if (b == 0) == (edge == 0) else inner)[x + a]
                    pieces += [first, first, second]
            forces.append(dot(left, jnp.concatenate(pieces, axis=0)) * lower[x])
        start = 8 if edge == 0 else 0
        for x in range(nx):
            total = forces[x + 1][start : start + 8] + forces[x][start + 16 : start + 24]
            force = gathered_force(total)
            rest = slice(1, ny - 1)
            for comp in range(3):
                scaled = HALF * inv_mass[x, node_y : node_y + 1] * force[comp : comp + 1]
                out[comp, x, node_y : node_y + 1] = rock[comp, x, node_y : node_y + 1] - scaled
                if edge == 0:
                    out[comp, x, rest] = rock[comp, x, rest]


def final_kernel(
    peers,
    members,
    info,
    pairs,
    family,
    mate_in,
    entries,
    rock,
    inv_mass,
    tails_in,
    values_in,
    sums_in,
    own,
    even_side,
    odd_side,
    pd_vel,
    fem_out,
    pd_out,
    table_ref,
    sums_ref,
):
    nx, ny, nz = inv_mass.shape
    width = peers * CAP
    tail_blocks = width // BLOCK
    blocks = sums_in.shape[0]
    table = blocks + tail_blocks
    place = info[0]
    core = place & 1
    for block in range(blocks):
        first = side_table(even_side, block)
        second = side_table(odd_side, block)
        before, after = neighbours(peers, place, first, second)
        table_ref[block] = before
        table_ref[table + block] = side_table(own, block)
        table_ref[2 * table + block] = after
        sums_ref[block] = sums_in[block]
    table_ref[3 * table] = jnp.zeros((8, BLOCK), F32)

    entry = entries[...]
    count = entry.shape[1]
    odd_owner, row, pick = entry_places(entry, blocks)
    tails, values = received(mate_in, peers, blocks, place, 1 - core, odd_owner != core, row, pick)
    tails = [tails[side] + tails_in[side] for side in range(3)]
    on = (jnp.where(place > 0, 1.0, 0.0), 1.0, jnp.where(place < peers - 1, 1.0, 0.0))
    for side in range(3):
        for tile in range(tail_blocks):
            part = tails[side][0:8, tile * BLOCK : (tile + 1) * BLOCK]
            table_ref[side * table + blocks + tile] = part * on[side]
    tail_rows = tails[1]

    def several(codes):
        ready = []
        for block, member in codes:
            left, sums = other_features(table_ref[member])
            ready.append((block, sums, pair_weights(left, own_features(table_ref[table + block]))))
        return [(block, fold(weighted(sums, weights))) for block, sums, weights in ready]

    for block in range(blocks, table):
        results = several([(block, family[k, block]) for k in range(members)])
        sums_ref[block] = sum((total for _, total in results[1:]), results[0][1])

    def some(index, carry):
        codes = [pairs[1 + BATCH * index + k] for k in range(BATCH)]
        for block, total in several([(code >> PAIR_SHIFT, code & ((1 << PAIR_SHIFT) - 1)) for code in codes]):
            sums_ref[block] = sums_ref[block] + total
        return carry

    node = entry[6:7].astype(jnp.int32)
    z_hot = one_hot(iota((nz, count), 0) == (node & (nz - 1)))
    xy_hit = iota((nx * ny, count), 0) == (node >> shift_of(nz))
    spread = []
    for comp in range(3):
        value = values[comp] + values_in[comp : comp + 1]
        spread.append(jnp.where(xy_hit, entry[3:4] * (entry[comp : comp + 1] - value), 0.0))
    pull = dot3_nt(jnp.concatenate(spread, axis=0), z_hot).reshape(3, nx, ny, nz)
    fem_out[...] = rock[...] - HALF * inv_mass[...][None] * pull

    stiff = tail_rows[14:15]
    target = tail_rows[15:16].astype(jnp.int32)
    hot_lane = one_hot(iota((BLOCK, width), 0) == (target & (BLOCK - 1)))
    target_block = target >> shift_of(BLOCK)
    tables = jnp.concatenate([side_table(own, block) for block in range(blocks)], axis=0)
    looked = dot3(tables, hot_lane)
    found = jnp.zeros((8, width), F32)
    for block in range(blocks):
        found = found + jnp.where(target_block == block, looked[8 * block : 8 * block + 8], 0.0)
    coupling = stiff * (tail_rows[11:14] - found[0:3])
    coupling = jnp.concatenate([coupling, jnp.zeros((5, width), F32)], axis=0)
    spread = jnp.concatenate([jnp.where(target_block == block, coupling, 0.0) for block in range(blocks)], axis=0)
    couple = dot3_nt(spread, hot_lane)

    lax.fori_loop(0, pairs[0], some, 0)

    scale = GAIN / (BLOCK * members)
    for block in range(table):
        total = sums_ref[block]
        points = table_ref[table + block]
        part = slice(block * BLOCK, (block + 1) * BLOCK)
        force = scale * points[3:4] * (total[0:3] - points[0:3] * total[3:4])
        if block < blocks:
            pd_out[:, part] = pd_vel[:, part] + HALF * (force + couple[8 * block : 8 * block + 3])
        else:
            tile = block - blocks
            pd_out[:, part] = tail_rows[8:11, tile * BLOCK : (tile + 1) * BLOCK] + HALF * force


def call(kernel, outs, specs, scratch, microseconds, args, name, out_specs=None, vmem=24):
    return pl.pallas_call(
        kernel,
        out_shape=outs,
        in_specs=specs,
        out_specs=out_specs or jax.tree.map(lambda _: VMEM, outs),
        scratch_shapes=scratch,
        compiler_params=params(vmem),
        cost_estimate=pl.CostEstimate(flops=0, bytes_accessed=int(3.6e6 * microseconds), transcendentals=0),
        name=name,
    )(*args)


def shards(
    fem_disp,
    fem_vel,
    modulus,
    inv_mass,
    element_stiffness,
    pd_pos,
    pd_disp,
    pd_vel,
    conv_state,
    conv_owner,
    family,
    ov_owner,
    ov_node,
    ov_target,
    ov_stiff,
):
    peers = lax.axis_size("lat")
    depth = lax.axis_size("depth")
    nx, ny, nz = modulus.shape
    blocks = pd_pos.shape[1] // BLOCK
    tail_blocks = peers * CAP // BLOCK
    table = blocks + tail_blocks
    members = family.shape[1]
    count = ov_node.shape[0]
    chips = peers // 2
    chunk_rows = 3 * blocks + 16 * tail_blocks
    shaped = jax.ShapeDtypeStruct
    info = jnp.stack([lax.axis_index("lat"), lax.axis_index("depth")]).astype(jnp.int32)

    both_faces = depth > 2
    family = family.T
    sources = (fem_disp, modulus, pd_pos, pd_disp)
    pay_even, pay_odd = call(
        side_kernel,
        (shaped((4 * blocks, nz), F32),) * 2,
        [FAR] * 4,
        [pltpu.VMEM(value.shape, value.dtype) for value in sources] + [pltpu.SemaphoreType.DMA((4,))],
        1.5,
        sources,
        "side",
        vmem=SIDE_VMEM,
    )
    swap = [(i, i ^ 1) for i in range(peers)]
    cross = [(i, i + 1) for i in range(1, peers - 1, 2)] + [(i + 1, i) for i in range(1, peers - 1, 2)]
    odd_side = lax.ppermute(pay_odd, "lat", cross)
    even_side = lax.ppermute(pay_even, "lat", swap)
    inputs = (
        fem_disp,
        pd_disp,
        conv_state,
        conv_owner.reshape(1, -1),
        ov_owner.reshape(1, -1),
        ov_node.reshape(1, -1),
        ov_target.reshape(1, -1),
        ov_stiff.reshape(1, -1),
    )
    chunk, entries = call(
        functools.partial(pack_kernel, peers),
        (shaped((chips, chunk_rows, BLOCK), F32), shaped((8, count), F32)),
        [VMEM] * 8,
        [pltpu.VMEM((chunk_rows, BLOCK), F32)],
        2.0,
        inputs,
        "pack",
    )
    chunk, even_side, odd_side = lax.optimization_barrier((chunk, even_side, odd_side))
    groups = [[side + 2 * k for k in range(chips)] for side in range(2)]
    mine = lax.all_to_all(chunk, "lat", split_axis=0, concat_axis=0, tiled=True, axis_index_groups=groups)

    count_faces = 2 if both_faces else 1
    faces = call(
        functools.partial(face_kernel, both_faces),
        shaped((count_faces, 4, ny + 2, nz), F32),
        [SMEM] + [VMEM] * 4,
        [],
        0.6,
        (info, fem_disp, modulus, even_side, odd_side),
        "face",
    )
    faces, pay_even, even_side, odd_side = lax.optimization_barrier((faces, pay_even, even_side, odd_side))
    if both_faces:
        low_x = lax.ppermute(faces[1], "depth", [(i, i + 1) for i in range(depth - 1)])
        high_x = lax.ppermute(faces[0], "depth", [(i + 1, i) for i in range(depth - 1)])
    else:
        low_x = high_x = lax.ppermute(faces[0], "depth", [(0, 1), (1, 0)])

    sums, pairs = call(
        functools.partial(bond_kernel, peers, tail_blocks, members),
        (shaped((blocks, 8, BLOCK), F32), shaped((table * members + BATCH + 1,), jnp.int32)),
        [SMEM, SMEM] + [VMEM] * 3 + [ANY],
        [pltpu.VMEM((3 * blocks + 1, BLOCK, 48), BF16), pltpu.VMEM((3 * blocks + 1, 32, BLOCK), BF16)],
        4.3,
        (info, family, pay_even, even_side, odd_side, faces),
        "bond",
        out_specs=(VMEM, SMEM),
    )
    node_rows = (nx + 2) * ny
    rock, edge_nodes, left = call(
        functools.partial(rock_kernel, depth),
        (shaped(fem_vel.shape, F32), shaped((2, nx + 2, 8, nz), F32), shaped((32, 192), BF16)),
        [SMEM] + [VMEM] * 7 + [ANY],
        [
            pltpu.VMEM((nz // BLOCK, node_rows * 8, BLOCK), F32),
            pltpu.VMEM((node_rows, 16, nz), BF16),
            pltpu.VMEM((node_rows, 16, nz), BF16),
            pltpu.VMEM((nz // BLOCK, nx * ny * 8, BLOCK), F32),
        ],
        1.8,
        (info, fem_disp, fem_vel, modulus, inv_mass, element_stiffness, low_x, high_x, sums),
        "rock",
    )
    mine, rock = lax.optimization_barrier((mine, rock))
    mate = lax.ppermute(mine, "lat", swap)
    rock, tails, values = call(
        functools.partial(edge_kernel, peers, depth, blocks),
        (shaped(fem_vel.shape, F32), shaped((3, 16, peers * CAP), F32), shaped((8, count), F32)),
        [SMEM] + [VMEM] * 10,
        [],
        1.0,
        (info, mine, entries, rock, inv_mass, edge_nodes, left, low_x, high_x, even_side, odd_side),
        "edge",
    )
    return call(
        functools.partial(final_kernel, peers, members),
        (shaped(fem_vel.shape, F32), shaped((3, table * BLOCK), F32)),
        [SMEM] * 3 + [VMEM] * 11,
        [pltpu.VMEM((3 * table + 1, 8, BLOCK), F32), pltpu.VMEM((table, 8, BLOCK), F32)],
        2.6,
        (
            info,
            pairs,
            family,
            mate,
            entries,
            rock,
            inv_mass,
            tails,
            values,
            sums,
            pay_even,
            even_side,
            odd_side,
            pd_vel,
        ),
        "final",
    )


def solution(mesh):
    lat = P(None, ("depth", "lat"))
    rows = P(("depth", "lat"), None)
    flat = P(("depth", "lat"))
    nodes = P(None, "depth", "lat", None)
    grid = P("depth", "lat", None)
    return jax.shard_map(
        shards,
        mesh=mesh,
        in_specs=(nodes, nodes, grid, grid, P(), lat, lat, lat, lat, rows, rows, rows, flat, flat, flat),
        out_specs=(nodes, lat),
        check_vma=False,
    )
```

```python
import functools
import math

import jax
import jax.numpy as jnp
from jax import lax
from jax.experimental import pallas as pl
from jax.experimental.pallas import tpu as pltpu
from jax.sharding import PartitionSpec as P

BLOCK = 128
CAP = 8
HALF = 0.5
GAIN = 8.0
LOG2E = math.log2(math.e)
F32 = jnp.float32
BF16 = jnp.bfloat16
LAG = 8
BATCH = 16
PAIR_SHIFT = 6
PAIR_SLOTS = 256
SIDE_VMEM = 63

VMEM = pl.BlockSpec(memory_space=pltpu.VMEM)
SMEM = pl.BlockSpec(memory_space=pltpu.SMEM)
FAR = pl.BlockSpec(memory_space=pltpu.HBM)
ANY = pl.BlockSpec(memory_space=pl.ANY)


def params(mebibytes):
    return pltpu.CompilerParams(vmem_limit_bytes=int(mebibytes * 1024 * 1024))


def split3(value):
    high = value.astype(BF16)
    rest = value - high.astype(F32)
    mid = rest.astype(BF16)
    low = (rest - mid.astype(F32)).astype(BF16)
    return high, mid, low


def dot(a, b):
    return jnp.dot(a, b, preferred_element_type=F32)


def dot_nt(a, b):
    return lax.dot_general(a, b, (((1,), (1,)), ((), ())), preferred_element_type=F32)


def dot3(value, hot):
    high, mid, low = split3(value)
    return (dot(high, hot) + dot(mid, hot)) + dot(low, hot)


def dot3_nt(value, hot):
    high, mid, low = split3(value)
    return (dot_nt(high, hot) + dot_nt(mid, hot)) + dot_nt(low, hot)


def iota(shape, axis):
    return lax.broadcasted_iota(jnp.int32, shape, axis)


def one_hot(condition):
    return jnp.where(condition, 1.0, 0.0).astype(BF16)


def shift_of(size):
    assert size & (size - 1) == 0
    return size.bit_length() - 1


def point_rows(pos, disp):
    norm = (-0.5 * LOG2E) * (pos[0:1] * pos[0:1] + pos[1:2] * pos[1:2] + pos[2:3] * pos[2:3])
    return jnp.concatenate([disp, jnp.ones_like(norm), pos, norm], axis=0)


def slots_of(owner_ref):
    named = owner_ref[...].astype(F32)
    rows = named.shape[1]
    wide = jnp.broadcast_to(named, (rows, rows))
    down, across = iota((rows, rows), 0), iota((rows, rows), 1)
    owner = jnp.sum(jnp.where(down == across, wide, 0.0), axis=1, keepdims=True)
    earlier = jnp.where((wide == owner) & (across < down), 1.0, 0.0)
    rank = jnp.sum(earlier, axis=1, keepdims=True)
    return owner * CAP + rank, named


def pack_kernel(
    peers,
    ov_node_in,
    fem_disp_in,
    conv_owner_in,
    ov_owner_in,
    conv_state_in,
    ov_target_in,
    ov_stiff_in,
    pd_disp_in,
    pd_pos_in,
    modulus_in,
    chunk,
    pay_even,
    pay_odd,
    rows_ref,
    ov_node,
    fem_disp,
    conv_owner,
    ov_owner,
    conv_state,
    ov_target,
    ov_stiff,
    pd_disp,
    pd_pos,
    modulus,
    sems,
):
    sources = (
        ov_node_in,
        fem_disp_in,
        conv_owner_in,
        ov_owner_in,
        conv_state_in,
        ov_target_in,
        ov_stiff_in,
        pd_disp_in,
        pd_pos_in,
        modulus_in,
    )
    places = (
        ov_node,
        fem_disp,
        conv_owner,
        ov_owner,
        conv_state,
        ov_target,
        ov_stiff,
        pd_disp,
        pd_pos,
        modulus,
    )
    copies = [pltpu.make_async_copy(f, t, sems.at[i]) for i, (f, t) in enumerate(zip(sources, places))]
    for copy in copies:
        copy.start()
    for copy in copies:
        copy.wait()
    _, nx, ny, nz = fem_disp.shape
    width = peers * CAP
    blocks = pd_disp.shape[1] // BLOCK
    count = ov_node.shape[1]
    node = ov_node[...]
    hot_z = one_hot(iota((nz, count), 0) == (node & (nz - 1)))
    picked = dot3(fem_disp[...].reshape(3 * nx * ny, nz), hot_z)
    hot_xy = jnp.where(iota((nx * ny, count), 0) == (node >> shift_of(nz)), 1.0, 0.0)
    at_node = jnp.sum(picked.reshape(3, nx * ny, count) * hot_xy[None], axis=1)
    conv_slot, _ = slots_of(conv_owner)
    ov_slot, ov_named = slots_of(ov_owner)
    lane = iota((conv_slot.shape[0], width), 1).astype(F32)
    state = conv_state[...]
    points = point_rows(state[0:3], state[3:6])
    blank = jnp.zeros((5, state.shape[1]), F32)
    conv_rows = jnp.concatenate([points, state[6:9], blank], axis=0)
    stiff = ov_stiff[...]
    target = ov_target[...].astype(F32)
    ov_rows = jnp.concatenate([jnp.zeros((3, count), F32), at_node, stiff, target], axis=0)
    conv_out = dot3(conv_rows, one_hot(conv_slot == lane))
    ov_out = dot3(ov_rows, one_hot(ov_slot == lane))
    pay_even[4 * blocks : 4 * blocks + 8, 0:count] = jnp.concatenate(
        [at_node, stiff, ov_named, target, node.astype(F32), jnp.zeros((1, count), F32)], axis=0
    )
    for block in range(blocks):
        for comp in range(3):
            rows_ref[comp * blocks + block : comp * blocks + block + 1] = pd_disp[
                comp : comp + 1, block * BLOCK : (block + 1) * BLOCK
            ]
    base = 3 * blocks
    for tile in range(width // BLOCK):
        part = slice(tile * BLOCK, (tile + 1) * BLOCK)
        rows_ref[base + 16 * tile : base + 16 * tile + 8] = conv_out[0:8, part]
        rows_ref[base + 16 * tile + 8 : base + 16 * tile + 16] = conv_out[8:16, part] + ov_out[:, part]
    value = rows_ref[...]
    for copy in range(chunk.shape[0]):
        chunk[copy] = value

    points = point_rows(pd_pos[...], pd_disp[...])
    for pair in range(blocks // 2):
        part = points[:, 2 * BLOCK * pair : 2 * BLOCK * (pair + 1)]
        pay_even[8 * pair : 8 * pair + 8] = part
        pay_odd[8 * pair : 8 * pair + 8] = part
    even = (lax.axis_index("lat") & 1) == 0
    for pay, top in ((pay_even, even), (pay_odd, jnp.logical_not(even))):
        row = jnp.where(top, ny - 1, 0)
        for x in range(nx):
            for comp in range(4):
                at = halo_row(4 * x + comp)
                pay[at : at + 1] = fem_disp[comp, x, pl.ds(row, 1)] if comp < 3 else modulus[x, pl.ds(row, 1)]


def halo_row(number):
    return 8 * (number // 2) + 3 + 4 * (number % 2)


def halo_rows(ref, x):
    return jnp.concatenate([ref[halo_row(4 * x + c) : halo_row(4 * x + c) + 1] for c in range(4)], axis=0)


def face_kernel(both_faces, info, fem_disp, modulus, even_side, odd_side, after, faces):
    nx, ny, nz = modulus.shape
    even = (info[0] & 1) == 0

    def rows_at(number):
        upper = halo_rows(even_side, number), halo_rows(odd_side, number)
        return jnp.where(even, upper[1], upper[0]), jnp.where(even, upper[0], upper[1])

    def put(face, chosen, low, high):
        for comp in range(4):
            faces[face, comp, 0:ny] = chosen(comp)
            faces[face, comp, ny : ny + 1] = low[comp : comp + 1]
            faces[face, comp, ny + 1 : ny + 2] = high[comp : comp + 1]

    def layer(number):
        return lambda comp: fem_disp[comp, number] if comp < 3 else modulus[number]

    if both_faces:
        for face, number in ((0, 0), (1, nx - 1)):
            put(face, layer(number), *rows_at(number))
    else:
        upper = info[1] == 0
        first, second = rows_at(nx - 1), rows_at(0)
        put(
            0,
            lambda comp: jnp.where(upper, layer(nx - 1)(comp), layer(0)(comp)),
            jnp.where(upper, first[0], second[0]),
            jnp.where(upper, first[1], second[1]),
        )


def side_table(ref, block):
    rows = ref[8 * (block // 2) : 8 * (block // 2) + 8, BLOCK * (block % 2) : BLOCK * (block % 2 + 1)]
    row = iota(rows.shape, 0)
    squares = jnp.where((row >= 4) & (row < 7), rows * rows, 0.0)
    norm = (-0.5 * LOG2E) * jnp.sum(squares, axis=0, keepdims=True)
    return jnp.where(row == 3, 1.0, jnp.where(row == 7, norm, rows))


def own_features(points):
    row = iota(points.shape, 0)
    turned = pltpu.roll(points, 4, 0)
    value = jnp.where(row == 3, turned, jnp.where(row < 3, 0.0, jnp.where(row == 7, 1.0, LOG2E * points)))
    high, mid, low = (part.astype(F32) for part in split3(value))
    return jnp.concatenate([high, mid, high, mid, low, high], axis=0).astype(BF16)


def other_features(points):
    high, mid, low = (part.astype(F32) for part in split3(points))
    left = jnp.concatenate([high, high, mid, mid, high, low], axis=0)
    sums = jnp.concatenate([high, mid, low, jnp.zeros_like(low)], axis=0)
    return left.astype(BF16).T, sums.astype(BF16)


def pair_weights(left, own):
    weight = jnp.exp2(dot(left, own))
    high = weight.astype(BF16)
    low = (weight - high.astype(F32)).astype(BF16)
    return jnp.concatenate([high, low], axis=0)


def weighted(sums, weights):
    return dot(jnp.concatenate([sums, sums], axis=1), weights)


def fold(total):
    return total[0:8] + total[8:16] + total[16:24]


def neighbours(peers, place, first, second):
    even = (place & 1) == 0
    before = jnp.where(place > 0, jnp.where(even, second, first), 0.0)
    return before, jnp.where(place < peers - 1, jnp.where(even, first, second), 0.0)


def member_codes(family, blocks, tail_blocks):
    table = blocks + tail_blocks
    side = (family >= table).astype(jnp.int32) + (family >= 2 * table).astype(jnp.int32)
    local = family - side * table
    outside = local >= blocks
    where = jnp.where(outside, 3 * blocks, side * blocks + local)
    is_tail = (outside & (family < 3 * table)).astype(jnp.int32)
    number = is_tail * (side * tail_blocks + local - blocks)
    return (((is_tail << PAIR_SHIFT) + number) << PAIR_SHIFT) + where


def low_bits(code):
    return code & ((1 << PAIR_SHIFT) - 1)


def bond_kernel(
    peers, tail_blocks, members, info, codes, own, even_side, odd_side, after, sums_out, tables, left_ref, sums_ref
):
    blocks = sums_out.shape[0]
    mine = []
    for block in range(blocks):
        first = side_table(even_side, block)
        second = side_table(odd_side, block)
        before, following = neighbours(peers, info[0], first, second)
        mine.append(side_table(own, block))
        for side, points in enumerate((before, mine[block], following)):
            left, sums = other_features(points)
            left_ref[side * blocks + block] = left
            sums_ref[side * blocks + block] = sums
            tables[side * blocks + block] = points
    left_ref[3 * blocks] = jnp.zeros(left_ref.shape[1:], BF16)
    sums_ref[3 * blocks] = jnp.zeros(sums_ref.shape[1:], BF16)
    tables[3 * blocks] = jnp.zeros(tables.shape[1:], F32)
    totals, places, weights = {}, {}, {}
    units = blocks * members

    for unit in range(units + LAG):
        if unit < units:
            block, k = divmod(unit, members)
            if k == 0:
                features = own_features(mine[block])
            code = codes[k, block]
            places[unit] = low_bits(code)
            weights[unit] = pair_weights(left_ref[places[unit]], features)
        if unit >= LAG:
            done = unit - LAG
            block, k = divmod(done, members)
            total = weighted(sums_ref[places[done]], weights.pop(done))
            totals[block] = total if k == 0 else totals[block] + total
            if k == members - 1:
                sums_out[block] = fold(totals.pop(block))


def list_tail_pairs(flat, pairs, tail_blocks):
    row = flat[...]
    count = row.shape[1]
    slots = pairs.shape[1]
    flags = (row >> (2 * PAIR_SHIFT)).astype(F32)
    entry = (row & ((1 << (2 * PAIR_SHIFT)) - 1)).astype(F32)
    down, across = iota((count, count), 0), iota((count, count), 1)
    wide = jnp.broadcast_to(flags, (count, count))
    rank = jnp.sum(jnp.where(across < down, wide, 0.0), axis=1, keepdims=True)
    mine = jnp.sum(jnp.where(across == down, wide, 0.0), axis=1, keepdims=True)
    lane = iota((count, slots), 1).astype(F32)
    listed = dot3(entry, one_hot((rank == lane) & (mine > 0.5)))
    found = jnp.sum(flags, axis=1, keepdims=True)
    slot = iota((1, slots), 1)
    listed = jnp.where(slot.astype(F32) < found, listed, 3.0 * tail_blocks).astype(jnp.int32)
    pairs[...] = jnp.where(slot == slots - 1, found.astype(jnp.int32), listed)


def stiffness_rows(stiffness):
    new, old = iota((32, 24), 0), iota((32, 24), 1)
    place = sum(
        jnp.where(old == k, (k // 3 // 2) * 8 + (k // 3 % 2) * 4 + k % 3, 0) for k in range(24)
    )
    hot = one_hot(new == place)
    parts = [dot_nt(dot(hot, part).astype(BF16), hot) for part in split3(stiffness)]
    high, mid, low = parts
    pieces = []
    for corner in range(4):
        part = slice(8 * corner, 8 * corner + 8)
        for piece in (high, high, mid, mid, high, low):
            pieces.append(piece[:, part])
    return jnp.concatenate(pieces, axis=1).astype(BF16)


def ahead(value):
    last = value.shape[1] - 1
    return jnp.where(iota(value.shape, 1) == last, 0.0, pltpu.roll(value, last, 1))


def node_parts(node):
    row = iota(node.shape, 0)
    value = jnp.where((row != 3) & (row != 7), node, 0.0)
    high, mid, low = (part.astype(F32) for part in split3(value))
    first = jnp.concatenate([high, mid], axis=0).astype(BF16)
    return first, jnp.concatenate([low, high], axis=0).astype(BF16)


def gathered_force(total):
    turned = pltpu.roll(pltpu.roll(total, 4, 0), 1, 1)
    return total + jnp.where(iota(total.shape, 1) != 0, turned, 0.0)


def put_nodes(nodes, at, ny, fields, halves):
    for comp, value in enumerate(fields):
        shifted = ahead(value)
        for half, part in enumerate(halves):
            nodes[half, pl.ds(at + comp, ny, stride=8), :] = value[:, part]
            nodes[half, pl.ds(at + comp + 4, ny, stride=8), :] = shifted[:, part]


def take_tile(ref, at):
    return jnp.concatenate([ref[h, at : at + 8, :] for h in range(ref.shape[0])], axis=1)


def put_tile(ref, at, value):
    for half in range(ref.shape[0]):
        ref[half, at : at + 8, :] = value[:, half * BLOCK : (half + 1) * BLOCK]


def take_rows(ref, at, count):
    return jnp.concatenate([ref[h, pl.ds(at, count, stride=8), :] for h in range(ref.shape[0])], axis=1)


def rock_kernel(
    tail_blocks,
    flat,
    fem_disp,
    fem_vel,
    modulus,
    inv_mass,
    stiffness,
    out,
    edge_nodes,
    left_out,
    first_ref,
    second_ref,
    pairs,
    nodes,
    force_ref,
):
    nx, ny, nz = modulus.shape
    list_tail_pairs(flat, pairs, tail_blocks)
    halves = [slice(h * BLOCK, (h + 1) * BLOCK) for h in range(nz // BLOCK)]
    left = stiffness_rows(stiffness[...])
    left_out[...] = left
    for x in range(nx):
        put_nodes(nodes, x * ny * 8, ny, [fem_disp[0, x], fem_disp[1, x], fem_disp[2, x], modulus[x]], halves)
    for x in range(nx):
        for y in range(ny):
            at = x * ny + y
            node = take_tile(nodes, 8 * at)
            if y in (0, ny - 1):
                edge_nodes[0 if y == 0 else 1, x] = node
            first_ref[at], second_ref[at] = node_parts(node)

    def element(x, y):
        pieces = []
        for a in range(2):
            for b in range(2):
                at = (x + a) * ny + y + b
                pieces += [first_ref[at], first_ref[at], second_ref[at]]
        return dot(left, jnp.concatenate(pieces, axis=0)) * take_tile(nodes, 8 * (x * ny + y))[3:4]

    before = None
    for x in range(nx):
        line = [element(x, y) for y in range(ny - 1)] if x < nx - 1 else None
        for y in range(ny):
            terms = []
            if line and y < ny - 1:
                terms.append(line[y][0:8])
            if line and y > 0:
                terms.append(line[y - 1][8:16])
            if before and y < ny - 1:
                terms.append(before[y][16:24])
            if before and y > 0:
                terms.append(before[y - 1][24:32])
            put_tile(force_ref, (x * ny + y) * 8, gathered_force(sum(terms[1:], terms[0])))
        before = line
    for x in range(nx):
        for comp in range(3):
            force = take_rows(force_ref, x * ny * 8 + comp, ny)
            out[comp, x] = fem_vel[comp, x] - HALF * inv_mass[x] * force


def outer_kernel(
    depth,
    info,
    rock,
    inv_mass,
    modulus,
    left_in,
    first_in,
    second_in,
    low_x,
    high_x,
    after,
    out,
    edge_nodes,
    nodes,
    first_ref,
    second_ref,
    force_ref,
):
    nx, ny, nz = inv_mass.shape
    halves = [slice(h * BLOCK, (h + 1) * BLOCK) for h in range(nz // BLOCK)]
    left = left_in[...]
    on = (jnp.where(info[1] > 0, 1.0, 0.0), jnp.where(info[1] < depth - 1, 1.0, 0.0))
    for side, face in enumerate((low_x, high_x)):
        put_nodes(nodes, side * ny * 8, ny, [face[comp, 0:ny] * on[side] for comp in range(4)], halves)
    for side in range(2):
        for y in range(ny):
            at = side * ny + y
            node = take_tile(nodes, 8 * at)
            if y in (0, ny - 1):
                edge_nodes[0 if y == 0 else 1, side] = node
            first_ref[at], second_ref[at] = node_parts(node)

    def inner(y, side):
        at = (nx - 1 if side else 0) * ny + y
        return first_in[at], second_in[at]

    def outer(y, side):
        return first_ref[side * ny + y], second_ref[side * ny + y]

    for side in range(2):
        line = []
        for y in range(ny - 1):
            pieces = []
            for a in range(2):
                for b in range(2):
                    first, second = (inner if a != side else outer)(y + b, side)
                    pieces += [first, first, second]
            mod = modulus[nx - 1, y : y + 1] if side else take_tile(nodes, 8 * y)[3:4]
            line.append(dot(left, jnp.concatenate(pieces, axis=0)) * mod)
        start = 0 if side else 16
        for y in range(ny):
            terms = []
            if y < ny - 1:
                terms.append(line[y][start : start + 8])
            if y > 0:
                terms.append(line[y - 1][start + 8 : start + 16])
            put_tile(force_ref, (side * ny + y) * 8, gathered_force(sum(terms[1:], terms[0])))
    for x in range(nx):
        for comp in range(3):
            value = rock[comp, x]
            if x in (0, nx - 1):
                side = 0 if x == 0 else 1
                value = value - HALF * inv_mass[x] * take_rows(force_ref, side * ny * 8 + comp, ny)
            out[comp, x] = value


def received(ref, peers, blocks, place, odd, wanted, row, pick):
    width = peers * CAP
    base = 3 * blocks

    def slot_rows(k):
        tiles = [ref[k, base + 16 * t : base + 16 * t + 16, :] for t in range(width // BLOCK)]
        return tiles[0] if len(tiles) == 1 else jnp.concatenate(tiles, axis=1)

    lane = iota((16, width), 1)
    back = lax.rem(width - CAP * (place - 1) + width, width)
    gathered = [jnp.zeros((16, width), F32) for _ in range(3)]
    for k in range(peers // 2):
        turned = pltpu.roll(slot_rows(k), back, 1)
        for side in range(3):
            window = jnp.where((lane >= CAP * side) & (lane < CAP * side + CAP), turned, 0.0)
            amount = (2 * CAP * k - CAP * side) % width
            gathered[side] = gathered[side] + (pltpu.roll(window, amount, 1) if amount else window)
    tails = [pltpu.roll(part, CAP * odd, 1) for part in gathered]
    rows = peers // 2 * blocks
    hit = (iota((rows, pick.shape[1]), 0) == row) & wanted
    looked = dot3(ref[:, 0:base, :].reshape(peers // 2 * base, BLOCK), pick)
    looked = looked.reshape(peers // 2, base, pick.shape[1])
    values = []
    for comp in range(3):
        got = looked[:, comp * blocks : (comp + 1) * blocks, :].reshape(rows, pick.shape[1])
        values.append(jnp.sum(jnp.where(hit, got, 0.0), axis=0, keepdims=True))
    return tails, values


def entry_rows(side, blocks, count):
    return side[4 * blocks : 4 * blocks + 8, 0:count]


def entry_places(entry, blocks):
    owner = entry[4:5].astype(jnp.int32)
    goal = entry[5:6].astype(jnp.int32)
    pick = one_hot(iota((BLOCK, entry.shape[1]), 0) == (goal & (BLOCK - 1)))
    return owner & 1, (owner >> 1) * blocks + (goal >> shift_of(BLOCK)), pick


def edge_kernel(
    peers,
    depth,
    blocks,
    info,
    mine_in,
    own_side,
    rock,
    inv_mass,
    edge_nodes,
    outer_nodes,
    left_in,
    low_x,
    high_x,
    even_side,
    odd_side,
    out,
    tails_out,
    values_out,
):
    nx, ny, nz = inv_mass.shape
    place = info[0]
    core = place & 1
    even = core == 0
    entry = entry_rows(own_side, blocks, values_out.shape[1])
    odd_owner, row, pick = entry_places(entry, blocks)
    tails, values = received(mine_in, peers, blocks, place, core, odd_owner == core, row, pick)
    for side in range(3):
        tails_out[side] = tails[side]
    values_out[...] = jnp.concatenate(values + [jnp.zeros((5, entry.shape[1]), F32)], axis=0)

    left = left_in[...]
    low_on = jnp.where(info[1] > 0, 1.0, 0.0)
    high_on = jnp.where(info[1] < depth - 1, 1.0, 0.0)
    for edge, from_even, node_y in ((0, jnp.logical_not(even), 0), (1, even, ny - 1)):
        inner, outer, lower = [], [], []
        for x in range(nx + 2):
            if x == 0:
                value = low_x[:, ny + edge] * low_on
            elif x == nx + 1:
                value = high_x[:, ny + edge] * high_on
            else:
                value = jnp.where(from_even, halo_rows(even_side, x - 1), halo_rows(odd_side, x - 1))
            other = jnp.concatenate([value, ahead(value)], axis=0)
            node = outer_nodes[edge, x // (nx + 1)] if x in (0, nx + 1) else edge_nodes[edge, x - 1]
            lower.append((other if edge == 0 else node)[3:4])
            inner.append(node_parts(node))
            outer.append(node_parts(other))
        forces = []
        for x in range(nx + 1):
            pieces = []
            for a in range(2):
                for b in range(2):
                    first, second = (outer if (b == 0) == (edge == 0) else inner)[x + a]
                    pieces += [first, first, second]
            forces.append(dot(left, jnp.concatenate(pieces, axis=0)) * lower[x])
        start = 8 if edge == 0 else 0
        for x in range(nx):
            total = forces[x + 1][start : start + 8] + forces[x][start + 16 : start + 24]
            force = gathered_force(total)
            rest = slice(1, ny - 1)
            for comp in range(3):
                scaled = HALF * inv_mass[x, node_y : node_y + 1] * force[comp : comp + 1]
                out[comp, x, node_y : node_y + 1] = rock[comp, x, node_y : node_y + 1] - scaled
                if edge == 0:
                    out[comp, x, rest] = rock[comp, x, rest]


def final_kernel(
    peers,
    members,
    info,
    pairs,
    codes,
    mate_in,
    own_side,
    rock,
    inv_mass,
    tails_in,
    values_in,
    sums_in,
    tables,
    pd_vel,
    fem_out,
    pd_out,
    sums_ref,
    own,
    tail_left,
    tail_sums,
):
    nx, ny, nz = inv_mass.shape
    width = peers * CAP
    tail_blocks = width // BLOCK
    blocks = sums_in.shape[0]
    table = blocks + tail_blocks
    place = info[0]
    core = place & 1
    for block in range(blocks):
        sums_ref[block] = sums_in[block]
        own[block] = tables[blocks + block]

    count = values_in.shape[1]
    entry = entry_rows(own_side, blocks, count)
    odd_owner, row, pick = entry_places(entry, blocks)
    tails, values = received(mate_in, peers, blocks, place, 1 - core, odd_owner != core, row, pick)
    tails = [tails[side] + tails_in[side] for side in range(3)]
    on = (jnp.where(place > 0, 1.0, 0.0), 1.0, jnp.where(place < peers - 1, 1.0, 0.0))
    for side in range(3):
        for tile in range(tail_blocks):
            points = tails[side][0:8, tile * BLOCK : (tile + 1) * BLOCK] * on[side]
            tail_left[side * tail_blocks + tile], tail_sums[side * tail_blocks + tile] = other_features(points)
            if side == 1:
                own[blocks + tile] = points
    tail_left[3 * tail_blocks] = jnp.zeros(tail_left.shape[1:], BF16)
    tail_sums[3 * tail_blocks] = jnp.zeros(tail_sums.shape[1:], BF16)
    tail_rows = tails[1]

    for tile in range(tail_blocks):
        block = blocks + tile
        features = own_features(own[block])
        ready = []
        for k in range(members):
            left, rows = other_features(tables[low_bits(codes[k, block])])
            ready.append((rows, pair_weights(left, features)))
        results = [weighted(rows, weights) for rows, weights in ready]
        sums_ref[block] = fold(sum(results[1:], results[0]))

    def some(index, carry):
        ready = []
        for k in range(BATCH):
            code = pairs[0, BATCH * index + k]
            block, number = code >> PAIR_SHIFT, low_bits(code)
            weights = pair_weights(tail_left[number], own_features(own[block]))
            ready.append((block, tail_sums[number], weights))
        results = [(block, fold(weighted(rows, weights))) for block, rows, weights in ready]
        for block, total in results:
            sums_ref[block] = sums_ref[block] + total
        return carry

    node = entry[6:7].astype(jnp.int32)
    z_hot = one_hot(iota((nz, count), 0) == (node & (nz - 1)))
    xy_hit = iota((nx * ny, count), 0) == (node >> shift_of(nz))
    spread = []
    for comp in range(3):
        value = values[comp] + values_in[comp : comp + 1]
        spread.append(jnp.where(xy_hit, entry[3:4] * (entry[comp : comp + 1] - value), 0.0))
    pull = dot3_nt(jnp.concatenate(spread, axis=0), z_hot).reshape(3, nx, ny, nz)
    fem_out[...] = rock[...] - HALF * inv_mass[...][None] * pull

    stiff = tail_rows[14:15]
    target = tail_rows[15:16].astype(jnp.int32)
    hot_lane = one_hot(iota((BLOCK, width), 0) == (target & (BLOCK - 1)))
    target_block = target >> shift_of(BLOCK)
    looked = dot3(tables[blocks : 2 * blocks].reshape(blocks * 8, BLOCK), hot_lane)
    found = jnp.zeros((8, width), F32)
    for block in range(blocks):
        found = found + jnp.where(target_block == block, looked[8 * block : 8 * block + 8], 0.0)
    coupling = stiff * (tail_rows[11:14] - found[0:3])
    coupling = jnp.concatenate([coupling, jnp.zeros((5, width), F32)], axis=0)
    spread = jnp.concatenate([jnp.where(target_block == block, coupling, 0.0) for block in range(blocks)], axis=0)
    couple = dot3_nt(spread, hot_lane)

    lax.fori_loop(0, (pairs[0, PAIR_SLOTS - 1] + BATCH - 1) // BATCH, some, 0)

    scale = GAIN / (BLOCK * members)
    for block in range(table):
        total = sums_ref[block]
        points = own[block]
        part = slice(block * BLOCK, (block + 1) * BLOCK)
        force = scale * points[3:4] * (total[0:3] - points[0:3] * total[3:4])
        if block < blocks:
            pd_out[:, part] = pd_vel[:, part] + HALF * (force + couple[8 * block : 8 * block + 3])
        else:
            tile = block - blocks
            pd_out[:, part] = tail_rows[8:11, tile * BLOCK : (tile + 1) * BLOCK] + HALF * force


def call(kernel, outs, specs, scratch, microseconds, args, name, out_specs=None, vmem=24):
    return pl.pallas_call(
        kernel,
        out_shape=outs,
        in_specs=specs,
        out_specs=out_specs or jax.tree.map(lambda _: VMEM, outs),
        scratch_shapes=scratch,
        compiler_params=params(vmem),
        cost_estimate=pl.CostEstimate(flops=0, bytes_accessed=int(3.6e6 * microseconds), transcendentals=0),
        name=name,
    )(*args)


def shards(
    fem_disp,
    fem_vel,
    modulus,
    inv_mass,
    element_stiffness,
    pd_pos,
    pd_disp,
    pd_vel,
    conv_state,
    conv_owner,
    family,
    ov_owner,
    ov_node,
    ov_target,
    ov_stiff,
):
    peers = lax.axis_size("lat")
    depth = lax.axis_size("depth")
    nx, ny, nz = modulus.shape
    blocks = pd_pos.shape[1] // BLOCK
    tail_blocks = peers * CAP // BLOCK
    table = blocks + tail_blocks
    members = family.shape[1]
    count = ov_node.shape[0]
    chips = peers // 2
    chunk_rows = 3 * blocks + 16 * tail_blocks
    shaped = jax.ShapeDtypeStruct
    info = jnp.stack([lax.axis_index("lat"), lax.axis_index("depth")]).astype(jnp.int32)

    both_faces = depth > 2
    family = family.T
    inputs = (
        ov_node.reshape(1, -1),
        fem_disp,
        conv_owner.reshape(1, -1),
        ov_owner.reshape(1, -1),
        conv_state,
        ov_target.reshape(1, -1),
        ov_stiff.reshape(1, -1),
        pd_disp,
        pd_pos,
        modulus,
    )
    chunk, pay_even, pay_odd = call(
        functools.partial(pack_kernel, peers),
        (
            shaped((chips, chunk_rows, BLOCK), F32),
            shaped((4 * blocks + 8, nz), F32),
            shaped((4 * blocks, nz), F32),
        ),
        [FAR] * 10,
        [pltpu.VMEM((chunk_rows, BLOCK), F32)]
        + [pltpu.VMEM(value.shape, value.dtype) for value in inputs]
        + [pltpu.SemaphoreType.DMA((10,))],
        2.6,
        inputs,
        "pack",
        vmem=SIDE_VMEM,
    )
    swap = [(i, i ^ 1) for i in range(peers)]
    cross = [(i, i + 1) for i in range(1, peers - 1, 2)] + [(i + 1, i) for i in range(1, peers - 1, 2)]
    odd_side = lax.ppermute(pay_odd, "lat", cross)
    even_side = lax.ppermute(pay_even, "lat", swap)
    groups = [[side + 2 * k for k in range(chips)] for side in range(2)]
    mine = lax.all_to_all(chunk, "lat", split_axis=0, concat_axis=0, tiled=True, axis_index_groups=groups)

    node_count = nx * ny
    codes = member_codes(family, blocks, tail_blocks)
    block_of = jnp.arange(table, dtype=jnp.int32)[None, :]
    flat = codes >> PAIR_SHIFT
    flat = ((flat >> PAIR_SHIFT) << (2 * PAIR_SHIFT)) + (block_of << PAIR_SHIFT) + low_bits(flat)
    rock, edge_nodes, left, first_parts, second_parts, pairs = call(
        functools.partial(rock_kernel, tail_blocks),
        (
            shaped(fem_vel.shape, F32),
            shaped((2, nx, 8, nz), F32),
            shaped((32, 192), BF16),
            shaped((node_count, 16, nz), BF16),
            shaped((node_count, 16, nz), BF16),
            shaped((1, PAIR_SLOTS), jnp.int32),
        ),
        [VMEM] * 6,
        [
            pltpu.VMEM((nz // BLOCK, node_count * 8, BLOCK), F32),
            pltpu.VMEM((nz // BLOCK, node_count * 8, BLOCK), F32),
        ],
        1.2,
        (flat.reshape(1, -1), fem_disp, fem_vel, modulus, inv_mass, element_stiffness),
        "rock",
    )
    count_faces = 2 if both_faces else 1
    rows = jnp.stack([even_side[: 4 * blocks], odd_side]).reshape(2, blocks // 2, 2, 4, nz)[:, :, :, 3]
    rows = rows.reshape(2, blocks, nz)[:, : 4 * nx].reshape(2, nx, 4, nz)
    even = (info[0] & 1) == 0
    ends = jnp.stack([jnp.where(even, rows[1], rows[0]), jnp.where(even, rows[0], rows[1])], axis=2)
    own = jnp.concatenate([fem_disp, modulus[None]], axis=0)
    layers = [jnp.concatenate([own[:, x], ends[x]], axis=1) for x in (0, nx - 1)]
    if both_faces:
        faces = jnp.stack(layers)
    else:
        faces = jnp.where(info[1] == 0, layers[1], layers[0])[None]
    faces, pay_even, even_side, odd_side = lax.optimization_barrier((faces, pay_even, even_side, odd_side))
    if both_faces:
        low_x = lax.ppermute(faces[1], "depth", [(i, i + 1) for i in range(depth - 1)])
        high_x = lax.ppermute(faces[0], "depth", [(i + 1, i) for i in range(depth - 1)])
    else:
        low_x = high_x = lax.ppermute(faces[0], "depth", [(0, 1), (1, 0)])

    sums, tables = call(
        functools.partial(bond_kernel, peers, tail_blocks, members),
        (
            shaped((blocks, 8, BLOCK), F32),
            shaped((3 * blocks + 1, 8, BLOCK), F32),
        ),
        [SMEM, SMEM] + [VMEM] * 3 + [ANY],
        [pltpu.VMEM((3 * blocks + 1, BLOCK, 48), BF16), pltpu.VMEM((3 * blocks + 1, 32, BLOCK), BF16)],
        4.3,
        (info, codes, pay_even, even_side, odd_side, faces),
        "bond",
    )
    mine, sums, low_x, high_x = lax.optimization_barrier((mine, sums, low_x, high_x))
    mate = lax.ppermute(mine, "lat", swap)
    rock, outer_nodes = call(
        functools.partial(outer_kernel, depth),
        (shaped(fem_vel.shape, F32), shaped((2, 2, 8, nz), F32)),
        [SMEM] + [VMEM] * 8 + [ANY],
        [
            pltpu.VMEM((nz // BLOCK, 2 * ny * 8, BLOCK), F32),
            pltpu.VMEM((2 * ny, 16, nz), BF16),
            pltpu.VMEM((2 * ny, 16, nz), BF16),
            pltpu.VMEM((nz // BLOCK, 2 * ny * 8, BLOCK), F32),
        ],
        0.8,
        (info, rock, inv_mass, modulus, left, first_parts, second_parts, low_x, high_x, sums),
        "outer",
    )
    rock, tails, values = call(
        functools.partial(edge_kernel, peers, depth, blocks),
        (shaped(fem_vel.shape, F32), shaped((3, 16, peers * CAP), F32), shaped((8, count), F32)),
        [SMEM] + [VMEM] * 11,
        [],
        1.0,
        (info, mine, pay_even, rock, inv_mass, edge_nodes, outer_nodes, left, low_x, high_x, even_side, odd_side),
        "edge",
    )
    return call(
        functools.partial(final_kernel, peers, members),
        (shaped(fem_vel.shape, F32), shaped((3, table * BLOCK), F32)),
        [SMEM] * 3 + [VMEM] * 9,
        [
            pltpu.VMEM((table, 8, BLOCK), F32),
            pltpu.VMEM((table, 8, BLOCK), F32),
            pltpu.VMEM((3 * tail_blocks + 1, BLOCK, 48), BF16),
            pltpu.VMEM((3 * tail_blocks + 1, 32, BLOCK), BF16),
        ],
        2.6,
        (info, pairs, codes, mate, pay_even, rock, inv_mass, tails, values, sums, tables, pd_vel),
        "final",
    )


def solution(mesh):
    lat = P(None, ("depth", "lat"))
    rows = P(("depth", "lat"), None)
    flat = P(("depth", "lat"))
    nodes = P(None, "depth", "lat", None)
    grid = P("depth", "lat", None)
    return jax.shard_map(
        shards,
        mesh=mesh,
        in_specs=(nodes, nodes, grid, grid, P(), lat, lat, lat, lat, rows, rows, rows, flat, flat, flat),
        out_specs=(nodes, lat),
        check_vma=False,
    )
```

```python
import functools
import math

import jax
import jax.numpy as jnp
from jax import lax
from jax.experimental import pallas as pl
from jax.experimental.pallas import tpu as pltpu
from jax.sharding import PartitionSpec as P

BLOCK = 128
CAP = 8
HALF = 0.5
GAIN = 8.0
LOG2E = math.log2(math.e)
F32 = jnp.float32
BF16 = jnp.bfloat16
LAG = 8
BATCH = 16
PAIR_SHIFT = 6
PAIR_SLOTS = 256
SIDE_VMEM = 63

VMEM = pl.BlockSpec(memory_space=pltpu.VMEM)
SMEM = pl.BlockSpec(memory_space=pltpu.SMEM)
FAR = pl.BlockSpec(memory_space=pltpu.HBM)
ANY = pl.BlockSpec(memory_space=pl.ANY)


def params(mebibytes):
    return pltpu.CompilerParams(vmem_limit_bytes=int(mebibytes * 1024 * 1024))


def split3(value):
    high = value.astype(BF16)
    rest = value - high.astype(F32)
    mid = rest.astype(BF16)
    low = (rest - mid.astype(F32)).astype(BF16)
    return high, mid, low


def dot(a, b):
    return jnp.dot(a, b, preferred_element_type=F32)


def dot_nt(a, b):
    return lax.dot_general(a, b, (((1,), (1,)), ((), ())), preferred_element_type=F32)


def dot3(value, hot):
    high, mid, low = split3(value)
    return (dot(high, hot) + dot(mid, hot)) + dot(low, hot)


def dot3_nt(value, hot):
    high, mid, low = split3(value)
    return (dot_nt(high, hot) + dot_nt(mid, hot)) + dot_nt(low, hot)


def iota(shape, axis):
    return lax.broadcasted_iota(jnp.int32, shape, axis)


def one_hot(condition):
    return jnp.where(condition, 1.0, 0.0).astype(BF16)


def shift_of(size):
    assert size & (size - 1) == 0
    return size.bit_length() - 1


def point_rows(pos, disp):
    norm = (-0.5 * LOG2E) * (pos[0:1] * pos[0:1] + pos[1:2] * pos[1:2] + pos[2:3] * pos[2:3])
    return jnp.concatenate([disp, jnp.ones_like(norm), pos, norm], axis=0)


def slots_of(owner_ref):
    named = owner_ref[...].astype(F32)
    rows = named.shape[1]
    wide = jnp.broadcast_to(named, (rows, rows))
    down, across = iota((rows, rows), 0), iota((rows, rows), 1)
    owner = jnp.sum(jnp.where(down == across, wide, 0.0), axis=1, keepdims=True)
    earlier = jnp.where((wide == owner) & (across < down), 1.0, 0.0)
    rank = jnp.sum(earlier, axis=1, keepdims=True)
    return owner * CAP + rank, named


def pack_kernel(
    peers,
    ov_node_in,
    fem_disp_in,
    conv_owner_in,
    ov_owner_in,
    conv_state_in,
    ov_target_in,
    ov_stiff_in,
    pd_disp_in,
    pd_pos_in,
    modulus_in,
    chunk,
    pay_even,
    pay_odd,
    rows_ref,
    ov_node,
    fem_disp,
    conv_owner,
    ov_owner,
    conv_state,
    ov_target,
    ov_stiff,
    pd_disp,
    pd_pos,
    modulus,
    sems,
):
    sources = (
        ov_node_in,
        fem_disp_in,
        conv_owner_in,
        ov_owner_in,
        conv_state_in,
        ov_target_in,
        ov_stiff_in,
        pd_disp_in,
        pd_pos_in,
        modulus_in,
    )
    places = (
        ov_node,
        fem_disp,
        conv_owner,
        ov_owner,
        conv_state,
        ov_target,
        ov_stiff,
        pd_disp,
        pd_pos,
        modulus,
    )
    copies = [pltpu.make_async_copy(f, t, sems.at[i]) for i, (f, t) in enumerate(zip(sources, places))]
    for copy in copies:
        copy.start()
    for copy in copies:
        copy.wait()
    _, nx, ny, nz = fem_disp.shape
    width = peers * CAP
    blocks = pd_disp.shape[1] // BLOCK
    count = ov_node.shape[1]
    node = ov_node[...]
    hot_z = one_hot(iota((nz, count), 0) == (node & (nz - 1)))
    picked = dot3(fem_disp[...].reshape(3 * nx * ny, nz), hot_z)
    hot_xy = jnp.where(iota((nx * ny, count), 0) == (node >> shift_of(nz)), 1.0, 0.0)
    at_node = jnp.sum(picked.reshape(3, nx * ny, count) * hot_xy[None], axis=1)
    conv_slot, _ = slots_of(conv_owner)
    ov_slot, ov_named = slots_of(ov_owner)
    lane = iota((conv_slot.shape[0], width), 1).astype(F32)
    state = conv_state[...]
    points = point_rows(state[0:3], state[3:6])
    blank = jnp.zeros((5, state.shape[1]), F32)
    conv_rows = jnp.concatenate([points, state[6:9], blank], axis=0)
    stiff = ov_stiff[...]
    target = ov_target[...].astype(F32)
    ov_rows = jnp.concatenate([jnp.zeros((3, count), F32), at_node, stiff, target], axis=0)
    conv_out = dot3(conv_rows, one_hot(conv_slot == lane))
    ov_out = dot3(ov_rows, one_hot(ov_slot == lane))
    pay_even[4 * blocks : 4 * blocks + 8, 0:count] = jnp.concatenate(
        [at_node, stiff, ov_named, target, node.astype(F32), jnp.zeros((1, count), F32)], axis=0
    )
    for block in range(blocks):
        for comp in range(3):
            rows_ref[comp * blocks + block : comp * blocks + block + 1] = pd_disp[
                comp : comp + 1, block * BLOCK : (block + 1) * BLOCK
            ]
    base = 3 * blocks
    for tile in range(width // BLOCK):
        part = slice(tile * BLOCK, (tile + 1) * BLOCK)
        rows_ref[base + 16 * tile : base + 16 * tile + 8] = conv_out[0:8, part]
        rows_ref[base + 16 * tile + 8 : base + 16 * tile + 16] = conv_out[8:16, part] + ov_out[:, part]
    value = rows_ref[...]
    for copy in range(chunk.shape[0]):
        chunk[copy] = value

    points = point_rows(pd_pos[...], pd_disp[...])
    for pair in range(blocks // 2):
        part = points[:, 2 * BLOCK * pair : 2 * BLOCK * (pair + 1)]
        pay_even[8 * pair : 8 * pair + 8] = part
        pay_odd[8 * pair : 8 * pair + 8] = part
    even = (lax.axis_index("lat") & 1) == 0
    for pay, top in ((pay_even, even), (pay_odd, jnp.logical_not(even))):
        row = jnp.where(top, ny - 1, 0)
        for x in range(nx):
            for comp in range(4):
                at = halo_row(4 * x + comp)
                pay[at : at + 1] = fem_disp[comp, x, pl.ds(row, 1)] if comp < 3 else modulus[x, pl.ds(row, 1)]


def halo_row(number):
    return 8 * (number // 2) + 3 + 4 * (number % 2)


def halo_rows(ref, x):
    return jnp.concatenate([ref[halo_row(4 * x + c) : halo_row(4 * x + c) + 1] for c in range(4)], axis=0)


def face_kernel(both_faces, info, fem_disp, modulus, even_side, odd_side, after, faces):
    nx, ny, nz = modulus.shape
    even = (info[0] & 1) == 0

    def rows_at(number):
        upper = halo_rows(even_side, number), halo_rows(odd_side, number)
        return jnp.where(even, upper[1], upper[0]), jnp.where(even, upper[0], upper[1])

    def put(face, chosen, low, high):
        for comp in range(4):
            faces[face, comp, 0:ny] = chosen(comp)
            faces[face, comp, ny : ny + 1] = low[comp : comp + 1]
            faces[face, comp, ny + 1 : ny + 2] = high[comp : comp + 1]

    def layer(number):
        return lambda comp: fem_disp[comp, number] if comp < 3 else modulus[number]

    if both_faces:
        for face, number in ((0, 0), (1, nx - 1)):
            put(face, layer(number), *rows_at(number))
    else:
        upper = info[1] == 0
        first, second = rows_at(nx - 1), rows_at(0)
        put(
            0,
            lambda comp: jnp.where(upper, layer(nx - 1)(comp), layer(0)(comp)),
            jnp.where(upper, first[0], second[0]),
            jnp.where(upper, first[1], second[1]),
        )


def side_table(ref, block):
    rows = ref[8 * (block // 2) : 8 * (block // 2) + 8, BLOCK * (block % 2) : BLOCK * (block % 2 + 1)]
    row = iota(rows.shape, 0)
    squares = jnp.where((row >= 4) & (row < 7), rows * rows, 0.0)
    norm = (-0.5 * LOG2E) * jnp.sum(squares, axis=0, keepdims=True)
    return jnp.where(row == 3, 1.0, jnp.where(row == 7, norm, rows))


def own_features(points):
    row = iota(points.shape, 0)
    turned = pltpu.roll(points, 4, 0)
    value = jnp.where(row == 3, turned, jnp.where(row < 3, 0.0, jnp.where(row == 7, 1.0, LOG2E * points)))
    high, mid, low = (part.astype(F32) for part in split3(value))
    return jnp.concatenate([high, mid, high, mid, low, high], axis=0).astype(BF16)


def other_features(points):
    high, mid, low = (part.astype(F32) for part in split3(points))
    left = jnp.concatenate([high, high, mid, mid, high, low], axis=0)
    sums = jnp.concatenate([high, mid, low, jnp.zeros_like(low)], axis=0)
    return left.astype(BF16).T, sums.astype(BF16)


def pair_weights(left, own):
    weight = jnp.exp2(dot(left, own))
    high = weight.astype(BF16)
    low = (weight - high.astype(F32)).astype(BF16)
    return jnp.concatenate([high, low], axis=0)


def weighted(sums, weights):
    return dot(jnp.concatenate([sums, sums], axis=1), weights)


def fold(total):
    return total[0:8] + total[8:16] + total[16:24]


def neighbours(peers, place, first, second):
    even = (place & 1) == 0
    before = jnp.where(place > 0, jnp.where(even, second, first), 0.0)
    return before, jnp.where(place < peers - 1, jnp.where(even, first, second), 0.0)


def member_codes(family, blocks, tail_blocks):
    table = blocks + tail_blocks
    side = (family >= table).astype(jnp.int32) + (family >= 2 * table).astype(jnp.int32)
    local = family - side * table
    outside = local >= blocks
    where = jnp.where(outside, 3 * blocks, side * blocks + local)
    is_tail = (outside & (family < 3 * table)).astype(jnp.int32)
    number = is_tail * (side * tail_blocks + local - blocks)
    return (((is_tail << PAIR_SHIFT) + number) << PAIR_SHIFT) + where


def low_bits(code):
    return code & ((1 << PAIR_SHIFT) - 1)


def bond_kernel(
    peers, tail_blocks, members, info, codes, own, even_side, odd_side, flat, after, sums_out, tables, pairs, left_ref, sums_ref
):
    list_tail_pairs(flat, pairs, tail_blocks)
    blocks = sums_out.shape[0]
    mine = []
    for block in range(blocks):
        first = side_table(even_side, block)
        second = side_table(odd_side, block)
        before, following = neighbours(peers, info[0], first, second)
        mine.append(side_table(own, block))
        for side, points in enumerate((before, mine[block], following)):
            left, sums = other_features(points)
            left_ref[side * blocks + block] = left
            sums_ref[side * blocks + block] = sums
            tables[side * blocks + block] = points
    left_ref[3 * blocks] = jnp.zeros(left_ref.shape[1:], BF16)
    sums_ref[3 * blocks] = jnp.zeros(sums_ref.shape[1:], BF16)
    tables[3 * blocks] = jnp.zeros(tables.shape[1:], F32)
    totals, places, weights = {}, {}, {}
    units = blocks * members

    for unit in range(units + LAG):
        if unit < units:
            block, k = divmod(unit, members)
            if k == 0:
                features = own_features(mine[block])
            code = codes[k, block]
            places[unit] = low_bits(code)
            weights[unit] = pair_weights(left_ref[places[unit]], features)
        if unit >= LAG:
            done = unit - LAG
            block, k = divmod(done, members)
            total = weighted(sums_ref[places[done]], weights.pop(done))
            totals[block] = total if k == 0 else totals[block] + total
            if k == members - 1:
                sums_out[block] = fold(totals.pop(block))


def list_tail_pairs(flat, pairs, tail_blocks):
    row = flat[...]
    count = row.shape[1]
    slots = pairs.shape[1]
    flags = (row >> (2 * PAIR_SHIFT)).astype(F32)
    entry = (row & ((1 << (2 * PAIR_SHIFT)) - 1)).astype(F32)
    down, across = iota((count, count), 0), iota((count, count), 1)
    wide = jnp.broadcast_to(flags, (count, count))
    rank = jnp.sum(jnp.where(across < down, wide, 0.0), axis=1, keepdims=True)
    mine = jnp.sum(jnp.where(across == down, wide, 0.0), axis=1, keepdims=True)
    lane = iota((count, slots), 1).astype(F32)
    listed = dot3(entry, one_hot((rank == lane) & (mine > 0.5)))
    found = jnp.sum(flags, axis=1, keepdims=True)
    slot = iota((1, slots), 1)
    listed = jnp.where(slot.astype(F32) < found, listed, 3.0 * tail_blocks).astype(jnp.int32)
    pairs[...] = jnp.where(slot == slots - 1, found.astype(jnp.int32), listed)


def stiffness_rows(stiffness):
    new, old = iota((32, 24), 0), iota((32, 24), 1)
    place = sum(
        jnp.where(old == k, (k // 3 // 2) * 8 + (k // 3 % 2) * 4 + k % 3, 0) for k in range(24)
    )
    hot = one_hot(new == place)
    parts = [dot_nt(dot(hot, part).astype(BF16), hot) for part in split3(stiffness)]
    high, mid, low = parts
    pieces = []
    for corner in range(4):
        part = slice(8 * corner, 8 * corner + 8)
        for piece in (high, high, mid, mid, high, low):
            pieces.append(piece[:, part])
    return jnp.concatenate(pieces, axis=1).astype(BF16)


def ahead(value):
    last = value.shape[1] - 1
    return jnp.where(iota(value.shape, 1) == last, 0.0, pltpu.roll(value, last, 1))


def node_parts(node):
    row = iota(node.shape, 0)
    value = jnp.where((row != 3) & (row != 7), node, 0.0)
    high, mid, low = (part.astype(F32) for part in split3(value))
    first = jnp.concatenate([high, mid], axis=0).astype(BF16)
    return first, jnp.concatenate([low, high], axis=0).astype(BF16)


def gathered_force(total):
    turned = pltpu.roll(pltpu.roll(total, 4, 0), 1, 1)
    return total + jnp.where(iota(total.shape, 1) != 0, turned, 0.0)


def put_nodes(nodes, at, ny, fields, halves):
    for comp, value in enumerate(fields):
        shifted = ahead(value)
        for half, part in enumerate(halves):
            nodes[half, pl.ds(at + comp, ny, stride=8), :] = value[:, part]
            nodes[half, pl.ds(at + comp + 4, ny, stride=8), :] = shifted[:, part]


def take_tile(ref, at):
    return jnp.concatenate([ref[h, at : at + 8, :] for h in range(ref.shape[0])], axis=1)


def put_tile(ref, at, value):
    for half in range(ref.shape[0]):
        ref[half, at : at + 8, :] = value[:, half * BLOCK : (half + 1) * BLOCK]


def take_rows(ref, at, count):
    return jnp.concatenate([ref[h, pl.ds(at, count, stride=8), :] for h in range(ref.shape[0])], axis=1)


def rock_kernel(
    fem_disp,
    fem_vel,
    modulus,
    inv_mass,
    stiffness,
    out,
    edge_nodes,
    left_out,
    first_ref,
    second_ref,
    nodes,
    force_ref,
):
    nx, ny, nz = modulus.shape
    halves = [slice(h * BLOCK, (h + 1) * BLOCK) for h in range(nz // BLOCK)]
    left = stiffness_rows(stiffness[...])
    left_out[...] = left
    for x in range(nx):
        put_nodes(nodes, x * ny * 8, ny, [fem_disp[0, x], fem_disp[1, x], fem_disp[2, x], modulus[x]], halves)
    for x in range(nx):
        for y in range(ny):
            at = x * ny + y
            node = take_tile(nodes, 8 * at)
            if y in (0, ny - 1):
                edge_nodes[0 if y == 0 else 1, x] = node
            first_ref[at], second_ref[at] = node_parts(node)

    def element(x, y):
        pieces = []
        for a in range(2):
            for b in range(2):
                at = (x + a) * ny + y + b
                pieces += [first_ref[at], first_ref[at], second_ref[at]]
        return dot(left, jnp.concatenate(pieces, axis=0)) * take_tile(nodes, 8 * (x * ny + y))[3:4]

    before = None
    for x in range(nx):
        line = [element(x, y) for y in range(ny - 1)] if x < nx - 1 else None
        for y in range(ny):
            terms = []
            if line and y < ny - 1:
                terms.append(line[y][0:8])
            if line and y > 0:
                terms.append(line[y - 1][8:16])
            if before and y < ny - 1:
                terms.append(before[y][16:24])
            if before and y > 0:
                terms.append(before[y - 1][24:32])
            put_tile(force_ref, (x * ny + y) * 8, gathered_force(sum(terms[1:], terms[0])))
        before = line
    for x in range(nx):
        for comp in range(3):
            force = take_rows(force_ref, x * ny * 8 + comp, ny)
            out[comp, x] = fem_vel[comp, x] - HALF * inv_mass[x] * force


def outer_kernel(
    depth,
    info,
    rock,
    inv_mass,
    modulus,
    left_in,
    first_in,
    second_in,
    low_x,
    high_x,
    after,
    out,
    edge_nodes,
    nodes,
    first_ref,
    second_ref,
    force_ref,
):
    nx, ny, nz = inv_mass.shape
    halves = [slice(h * BLOCK, (h + 1) * BLOCK) for h in range(nz // BLOCK)]
    left = left_in[...]
    on = (jnp.where(info[1] > 0, 1.0, 0.0), jnp.where(info[1] < depth - 1, 1.0, 0.0))
    for side, face in enumerate((low_x, high_x)):
        put_nodes(nodes, side * ny * 8, ny, [face[comp, 0:ny] * on[side] for comp in range(4)], halves)
    for side in range(2):
        for y in range(ny):
            at = side * ny + y
            node = take_tile(nodes, 8 * at)
            if y in (0, ny - 1):
                edge_nodes[0 if y == 0 else 1, side] = node
            first_ref[at], second_ref[at] = node_parts(node)

    def inner(y, side):
        at = (nx - 1 if side else 0) * ny + y
        return first_in[at], second_in[at]

    def outer(y, side):
        return first_ref[side * ny + y], second_ref[side * ny + y]

    for side in range(2):
        line = []
        for y in range(ny - 1):
            pieces = []
            for a in range(2):
                for b in range(2):
                    first, second = (inner if a != side else outer)(y + b, side)
                    pieces += [first, first, second]
            mod = modulus[nx - 1, y : y + 1] if side else take_tile(nodes, 8 * y)[3:4]
            line.append(dot(left, jnp.concatenate(pieces, axis=0)) * mod)
        start = 0 if side else 16
        for y in range(ny):
            terms = []
            if y < ny - 1:
                terms.append(line[y][start : start + 8])
            if y > 0:
                terms.append(line[y - 1][start + 8 : start + 16])
            put_tile(force_ref, (side * ny + y) * 8, gathered_force(sum(terms[1:], terms[0])))
    for x in range(nx):
        for comp in range(3):
            value = rock[comp, x]
            if x in (0, nx - 1):
                side = 0 if x == 0 else 1
                value = value - HALF * inv_mass[x] * take_rows(force_ref, side * ny * 8 + comp, ny)
            out[comp, x] = value


def received(ref, peers, blocks, place, odd, wanted, row, pick):
    width = peers * CAP
    base = 3 * blocks

    def slot_rows(k):
        tiles = [ref[k, base + 16 * t : base + 16 * t + 16, :] for t in range(width // BLOCK)]
        return tiles[0] if len(tiles) == 1 else jnp.concatenate(tiles, axis=1)

    lane = iota((16, width), 1)
    back = lax.rem(width - CAP * (place - 1) + width, width)
    gathered = [jnp.zeros((16, width), F32) for _ in range(3)]
    for k in range(peers // 2):
        turned = pltpu.roll(slot_rows(k), back, 1)
        for side in range(3):
            window = jnp.where((lane >= CAP * side) & (lane < CAP * side + CAP), turned, 0.0)
            amount = (2 * CAP * k - CAP * side) % width
            gathered[side] = gathered[side] + (pltpu.roll(window, amount, 1) if amount else window)
    tails = [pltpu.roll(part, CAP * odd, 1) for part in gathered]
    rows = peers // 2 * blocks
    hit = (iota((rows, pick.shape[1]), 0) == row) & wanted
    looked = dot3(ref[:, 0:base, :].reshape(peers // 2 * base, BLOCK), pick)
    looked = looked.reshape(peers // 2, base, pick.shape[1])
    values = []
    for comp in range(3):
        got = looked[:, comp * blocks : (comp + 1) * blocks, :].reshape(rows, pick.shape[1])
        values.append(jnp.sum(jnp.where(hit, got, 0.0), axis=0, keepdims=True))
    return tails, values


def entry_rows(side, blocks, count):
    return side[4 * blocks : 4 * blocks + 8, 0:count]


def entry_places(entry, blocks):
    owner = entry[4:5].astype(jnp.int32)
    goal = entry[5:6].astype(jnp.int32)
    pick = one_hot(iota((BLOCK, entry.shape[1]), 0) == (goal & (BLOCK - 1)))
    return owner & 1, (owner >> 1) * blocks + (goal >> shift_of(BLOCK)), pick


def edge_kernel(
    peers,
    depth,
    blocks,
    info,
    mine_in,
    own_side,
    rock,
    inv_mass,
    edge_nodes,
    outer_nodes,
    left_in,
    low_x,
    high_x,
    even_side,
    odd_side,
    out,
    tails_out,
    values_out,
):
    nx, ny, nz = inv_mass.shape
    place = info[0]
    core = place & 1
    even = core == 0
    entry = entry_rows(own_side, blocks, values_out.shape[1])
    odd_owner, row, pick = entry_places(entry, blocks)
    tails, values = received(mine_in, peers, blocks, place, core, odd_owner == core, row, pick)
    for side in range(3):
        tails_out[side] = tails[side]
    values_out[...] = jnp.concatenate(values + [jnp.zeros((5, entry.shape[1]), F32)], axis=0)

    left = left_in[...]
    low_on = jnp.where(info[1] > 0, 1.0, 0.0)
    high_on = jnp.where(info[1] < depth - 1, 1.0, 0.0)
    for edge, from_even, node_y in ((0, jnp.logical_not(even), 0), (1, even, ny - 1)):
        inner, outer, lower = [], [], []
        for x in range(nx + 2):
            if x == 0:
                value = low_x[:, ny + edge] * low_on
            elif x == nx + 1:
                value = high_x[:, ny + edge] * high_on
            else:
                value = jnp.where(from_even, halo_rows(even_side, x - 1), halo_rows(odd_side, x - 1))
            other = jnp.concatenate([value, ahead(value)], axis=0)
            node = outer_nodes[edge, x // (nx + 1)] if x in (0, nx + 1) else edge_nodes[edge, x - 1]
            lower.append((other if edge == 0 else node)[3:4])
            inner.append(node_parts(node))
            outer.append(node_parts(other))
        forces = []
        for x in range(nx + 1):
            pieces = []
            for a in range(2):
                for b in range(2):
                    first, second = (outer if (b == 0) == (edge == 0) else inner)[x + a]
                    pieces += [first, first, second]
            forces.append(dot(left, jnp.concatenate(pieces, axis=0)) * lower[x])
        start = 8 if edge == 0 else 0
        for x in range(nx):
            total = forces[x + 1][start : start + 8] + forces[x][start + 16 : start + 24]
            force = gathered_force(total)
            rest = slice(1, ny - 1)
            for comp in range(3):
                scaled = HALF * inv_mass[x, node_y : node_y + 1] * force[comp : comp + 1]
                out[comp, x, node_y : node_y + 1] = rock[comp, x, node_y : node_y + 1] - scaled
                if edge == 0:
                    out[comp, x, rest] = rock[comp, x, rest]


def final_kernel(
    peers,
    members,
    info,
    pairs,
    codes,
    mate_in,
    own_side,
    rock,
    inv_mass,
    tails_in,
    values_in,
    sums_in,
    tables,
    pd_vel,
    fem_out,
    pd_out,
    sums_ref,
    own,
    tail_left,
    tail_sums,
):
    nx, ny, nz = inv_mass.shape
    width = peers * CAP
    tail_blocks = width // BLOCK
    blocks = sums_in.shape[0]
    table = blocks + tail_blocks
    place = info[0]
    core = place & 1
    for block in range(blocks):
        sums_ref[block] = sums_in[block]
        own[block] = tables[blocks + block]

    count = values_in.shape[1]
    entry = entry_rows(own_side, blocks, count)
    odd_owner, row, pick = entry_places(entry, blocks)
    tails, values = received(mate_in, peers, blocks, place, 1 - core, odd_owner != core, row, pick)
    tails = [tails[side] + tails_in[side] for side in range(3)]
    on = (jnp.where(place > 0, 1.0, 0.0), 1.0, jnp.where(place < peers - 1, 1.0, 0.0))
    for side in range(3):
        for tile in range(tail_blocks):
            points = tails[side][0:8, tile * BLOCK : (tile + 1) * BLOCK] * on[side]
            tail_left[side * tail_blocks + tile], tail_sums[side * tail_blocks + tile] = other_features(points)
            if side == 1:
                own[blocks + tile] = points
    tail_left[3 * tail_blocks] = jnp.zeros(tail_left.shape[1:], BF16)
    tail_sums[3 * tail_blocks] = jnp.zeros(tail_sums.shape[1:], BF16)
    tail_rows = tails[1]

    for tile in range(tail_blocks):
        block = blocks + tile
        features = own_features(own[block])
        ready = []
        for k in range(members):
            left, rows = other_features(tables[low_bits(codes[k, block])])
            ready.append((rows, pair_weights(left, features)))
        results = [weighted(rows, weights) for rows, weights in ready]
        sums_ref[block] = fold(sum(results[1:], results[0]))

    def some(index, carry):
        ready = []
        for k in range(BATCH):
            code = pairs[0, BATCH * index + k]
            block, number = code >> PAIR_SHIFT, low_bits(code)
            weights = pair_weights(tail_left[number], own_features(own[block]))
            ready.append((block, tail_sums[number], weights))
        results = [(block, fold(weighted(rows, weights))) for block, rows, weights in ready]
        for block, total in results:
            sums_ref[block] = sums_ref[block] + total
        return carry

    node = entry[6:7].astype(jnp.int32)
    z_hot = one_hot(iota((nz, count), 0) == (node & (nz - 1)))
    xy_hit = iota((nx * ny, count), 0) == (node >> shift_of(nz))
    spread = []
    for comp in range(3):
        value = values[comp] + values_in[comp : comp + 1]
        spread.append(jnp.where(xy_hit, entry[3:4] * (entry[comp : comp + 1] - value), 0.0))
    pull = dot3_nt(jnp.concatenate(spread, axis=0), z_hot).reshape(3, nx, ny, nz)
    fem_out[...] = rock[...] - HALF * inv_mass[...][None] * pull

    stiff = tail_rows[14:15]
    target = tail_rows[15:16].astype(jnp.int32)
    hot_lane = one_hot(iota((BLOCK, width), 0) == (target & (BLOCK - 1)))
    target_block = target >> shift_of(BLOCK)
    looked = dot3(tables[blocks : 2 * blocks].reshape(blocks * 8, BLOCK), hot_lane)
    found = jnp.zeros((8, width), F32)
    for block in range(blocks):
        found = found + jnp.where(target_block == block, looked[8 * block : 8 * block + 8], 0.0)
    coupling = stiff * (tail_rows[11:14] - found[0:3])
    coupling = jnp.concatenate([coupling, jnp.zeros((5, width), F32)], axis=0)
    spread = jnp.concatenate([jnp.where(target_block == block, coupling, 0.0) for block in range(blocks)], axis=0)
    couple = dot3_nt(spread, hot_lane)

    lax.fori_loop(0, (pairs[0, PAIR_SLOTS - 1] + BATCH - 1) // BATCH, some, 0)

    scale = GAIN / (BLOCK * members)
    for block in range(table):
        total = sums_ref[block]
        points = own[block]
        part = slice(block * BLOCK, (block + 1) * BLOCK)
        force = scale * points[3:4] * (total[0:3] - points[0:3] * total[3:4])
        if block < blocks:
            pd_out[:, part] = pd_vel[:, part] + HALF * (force + couple[8 * block : 8 * block + 3])
        else:
            tile = block - blocks
            pd_out[:, part] = tail_rows[8:11, tile * BLOCK : (tile + 1) * BLOCK] + HALF * force


def call(kernel, outs, specs, scratch, microseconds, args, name, out_specs=None, vmem=24):
    return pl.pallas_call(
        kernel,
        out_shape=outs,
        in_specs=specs,
        out_specs=out_specs or jax.tree.map(lambda _: VMEM, outs),
        scratch_shapes=scratch,
        compiler_params=params(vmem),
        cost_estimate=pl.CostEstimate(flops=0, bytes_accessed=int(3.6e6 * microseconds), transcendentals=0),
        name=name,
    )(*args)


def shards(
    fem_disp,
    fem_vel,
    modulus,
    inv_mass,
    element_stiffness,
    pd_pos,
    pd_disp,
    pd_vel,
    conv_state,
    conv_owner,
    family,
    ov_owner,
    ov_node,
    ov_target,
    ov_stiff,
):
    peers = lax.axis_size("lat")
    depth = lax.axis_size("depth")
    nx, ny, nz = modulus.shape
    blocks = pd_pos.shape[1] // BLOCK
    tail_blocks = peers * CAP // BLOCK
    table = blocks + tail_blocks
    members = family.shape[1]
    count = ov_node.shape[0]
    chips = peers // 2
    chunk_rows = 3 * blocks + 16 * tail_blocks
    shaped = jax.ShapeDtypeStruct
    info = jnp.stack([lax.axis_index("lat"), lax.axis_index("depth")]).astype(jnp.int32)

    both_faces = depth > 2
    family = family.T
    inputs = (
        ov_node.reshape(1, -1),
        fem_disp,
        conv_owner.reshape(1, -1),
        ov_owner.reshape(1, -1),
        conv_state,
        ov_target.reshape(1, -1),
        ov_stiff.reshape(1, -1),
        pd_disp,
        pd_pos,
        modulus,
    )
    chunk, pay_even, pay_odd = call(
        functools.partial(pack_kernel, peers),
        (
            shaped((chips, chunk_rows, BLOCK), F32),
            shaped((4 * blocks + 8, nz), F32),
            shaped((4 * blocks, nz), F32),
        ),
        [FAR] * 10,
        [pltpu.VMEM((chunk_rows, BLOCK), F32)]
        + [pltpu.VMEM(value.shape, value.dtype) for value in inputs]
        + [pltpu.SemaphoreType.DMA((10,))],
        2.6,
        inputs,
        "pack",
        vmem=SIDE_VMEM,
    )
    swap = [(i, i ^ 1) for i in range(peers)]
    cross = [(i, i + 1) for i in range(1, peers - 1, 2)] + [(i + 1, i) for i in range(1, peers - 1, 2)]
    odd_side = lax.ppermute(pay_odd, "lat", cross)
    even_side = lax.ppermute(pay_even, "lat", swap)
    groups = [[side + 2 * k for k in range(chips)] for side in range(2)]
    mine = lax.all_to_all(chunk, "lat", split_axis=0, concat_axis=0, tiled=True, axis_index_groups=groups)

    node_count = nx * ny
    codes = member_codes(family, blocks, tail_blocks)
    block_of = jnp.arange(table, dtype=jnp.int32)[None, :]
    flat = codes >> PAIR_SHIFT
    flat = ((flat >> PAIR_SHIFT) << (2 * PAIR_SHIFT)) + (block_of << PAIR_SHIFT) + low_bits(flat)
    rock, edge_nodes, left, first_parts, second_parts = call(
        rock_kernel,
        (
            shaped(fem_vel.shape, F32),
            shaped((2, nx, 8, nz), F32),
            shaped((32, 192), BF16),
            shaped((node_count, 16, nz), BF16),
            shaped((node_count, 16, nz), BF16),
        ),
        [VMEM] * 5,
        [
            pltpu.VMEM((nz // BLOCK, node_count * 8, BLOCK), F32),
            pltpu.VMEM((nz // BLOCK, node_count * 8, BLOCK), F32),
        ],
        1.2,
        (fem_disp, fem_vel, modulus, inv_mass, element_stiffness),
        "rock",
    )
    count_faces = 2 if both_faces else 1
    rows = jnp.stack([even_side[: 4 * blocks], odd_side]).reshape(2, blocks // 2, 2, 4, nz)[:, :, :, 3]
    rows = rows.reshape(2, blocks, nz)[:, : 4 * nx].reshape(2, nx, 4, nz)
    even = (info[0] & 1) == 0
    ends = jnp.stack([jnp.where(even, rows[1], rows[0]), jnp.where(even, rows[0], rows[1])], axis=2)
    own = jnp.concatenate([fem_disp, modulus[None]], axis=0)
    layers = [jnp.concatenate([own[:, x], ends[x]], axis=1) for x in (0, nx - 1)]
    if both_faces:
        faces = jnp.stack(layers)
    else:
        faces = jnp.where(info[1] == 0, layers[1], layers[0])[None]
    faces, pay_even, even_side, odd_side = lax.optimization_barrier((faces, pay_even, even_side, odd_side))
    if both_faces:
        low_x = lax.ppermute(faces[1], "depth", [(i, i + 1) for i in range(depth - 1)])
        high_x = lax.ppermute(faces[0], "depth", [(i + 1, i) for i in range(depth - 1)])
    else:
        low_x = high_x = lax.ppermute(faces[0], "depth", [(0, 1), (1, 0)])

    sums, tables, pairs = call(
        functools.partial(bond_kernel, peers, tail_blocks, members),
        (
            shaped((blocks, 8, BLOCK), F32),
            shaped((3 * blocks + 1, 8, BLOCK), F32),
            shaped((1, PAIR_SLOTS), jnp.int32),
        ),
        [SMEM, SMEM] + [VMEM] * 4 + [ANY],
        [pltpu.VMEM((3 * blocks + 1, BLOCK, 48), BF16), pltpu.VMEM((3 * blocks + 1, 32, BLOCK), BF16)],
        4.3,
        (info, codes, pay_even, even_side, odd_side, flat.reshape(1, -1), faces),
        "bond",
    )
    mine, sums, low_x, high_x = lax.optimization_barrier((mine, sums, low_x, high_x))
    mate = lax.ppermute(mine, "lat", swap)
    rock, outer_nodes = call(
        functools.partial(outer_kernel, depth),
        (shaped(fem_vel.shape, F32), shaped((2, 2, 8, nz), F32)),
        [SMEM] + [VMEM] * 8 + [ANY],
        [
            pltpu.VMEM((nz // BLOCK, 2 * ny * 8, BLOCK), F32),
            pltpu.VMEM((2 * ny, 16, nz), BF16),
            pltpu.VMEM((2 * ny, 16, nz), BF16),
            pltpu.VMEM((nz // BLOCK, 2 * ny * 8, BLOCK), F32),
        ],
        0.8,
        (info, rock, inv_mass, modulus, left, first_parts, second_parts, low_x, high_x, sums),
        "outer",
    )
    rock, tails, values = call(
        functools.partial(edge_kernel, peers, depth, blocks),
        (shaped(fem_vel.shape, F32), shaped((3, 16, peers * CAP), F32), shaped((8, count), F32)),
        [SMEM] + [VMEM] * 11,
        [],
        1.0,
        (info, mine, pay_even, rock, inv_mass, edge_nodes, outer_nodes, left, low_x, high_x, even_side, odd_side),
        "edge",
    )
    return call(
        functools.partial(final_kernel, peers, members),
        (shaped(fem_vel.shape, F32), shaped((3, table * BLOCK), F32)),
        [SMEM] * 3 + [VMEM] * 9,
        [
            pltpu.VMEM((table, 8, BLOCK), F32),
            pltpu.VMEM((table, 8, BLOCK), F32),
            pltpu.VMEM((3 * tail_blocks + 1, BLOCK, 48), BF16),
            pltpu.VMEM((3 * tail_blocks + 1, 32, BLOCK), BF16),
        ],
        2.6,
        (info, pairs, codes, mate, pay_even, rock, inv_mass, tails, values, sums, tables, pd_vel),
        "final",
    )


def solution(mesh):
    lat = P(None, ("depth", "lat"))
    rows = P(("depth", "lat"), None)
    flat = P(("depth", "lat"))
    nodes = P(None, "depth", "lat", None)
    grid = P("depth", "lat", None)
    return jax.shard_map(
        shards,
        mesh=mesh,
        in_specs=(nodes, nodes, grid, grid, P(), lat, lat, lat, lat, rows, rows, rows, flat, flat, flat),
        out_specs=(nodes, lat),
        check_vma=False,
    )
```

```python
import functools
import math

import jax
import jax.numpy as jnp
from jax import lax
from jax.experimental import pallas as pl
from jax.experimental.pallas import tpu as pltpu
from jax.sharding import PartitionSpec as P

BLOCK = 128
CAP = 8
HALF = 0.5
GAIN = 8.0
LOG2E = math.log2(math.e)
F32 = jnp.float32
BF16 = jnp.bfloat16
LAG = 8
BATCH = 16
PAIR_SHIFT = 6
PAIR_SLOTS = 256
SIDE_VMEM = 63

VMEM = pl.BlockSpec(memory_space=pltpu.VMEM)
SMEM = pl.BlockSpec(memory_space=pltpu.SMEM)
FAR = pl.BlockSpec(memory_space=pltpu.HBM)
ANY = pl.BlockSpec(memory_space=pl.ANY)


def params(mebibytes):
    return pltpu.CompilerParams(vmem_limit_bytes=int(mebibytes * 1024 * 1024))


def split3(value):
    high = value.astype(BF16)
    rest = value - high.astype(F32)
    mid = rest.astype(BF16)
    low = (rest - mid.astype(F32)).astype(BF16)
    return high, mid, low


def dot(a, b):
    return jnp.dot(a, b, preferred_element_type=F32)


def dot_nt(a, b):
    return lax.dot_general(a, b, (((1,), (1,)), ((), ())), preferred_element_type=F32)


def dot3(value, hot):
    high, mid, low = split3(value)
    return (dot(high, hot) + dot(mid, hot)) + dot(low, hot)


def dot3_nt(value, hot):
    high, mid, low = split3(value)
    return (dot_nt(high, hot) + dot_nt(mid, hot)) + dot_nt(low, hot)


def iota(shape, axis):
    return lax.broadcasted_iota(jnp.int32, shape, axis)


def one_hot(condition):
    return jnp.where(condition, 1.0, 0.0).astype(BF16)


def shift_of(size):
    assert size & (size - 1) == 0
    return size.bit_length() - 1


def point_rows(pos, disp):
    norm = (-0.5 * LOG2E) * (pos[0:1] * pos[0:1] + pos[1:2] * pos[1:2] + pos[2:3] * pos[2:3])
    return jnp.concatenate([disp, jnp.ones_like(norm), pos, norm], axis=0)


def slots_of(owner_ref):
    named = owner_ref[...].astype(F32)
    rows = named.shape[1]
    wide = jnp.broadcast_to(named, (rows, rows))
    down, across = iota((rows, rows), 0), iota((rows, rows), 1)
    owner = jnp.sum(jnp.where(down == across, wide, 0.0), axis=1, keepdims=True)
    earlier = jnp.where((wide == owner) & (across < down), 1.0, 0.0)
    rank = jnp.sum(earlier, axis=1, keepdims=True)
    return owner * CAP + rank, named


def pack_kernel(
    peers,
    ov_node_in,
    fem_disp_in,
    conv_owner_in,
    ov_owner_in,
    conv_state_in,
    ov_target_in,
    ov_stiff_in,
    pd_disp_in,
    pd_pos_in,
    modulus_in,
    chunk,
    pay_even,
    pay_odd,
    rows_ref,
    ov_node,
    fem_disp,
    conv_owner,
    ov_owner,
    conv_state,
    ov_target,
    ov_stiff,
    pd_disp,
    pd_pos,
    modulus,
    sems,
):
    sources = (
        ov_node_in,
        fem_disp_in,
        conv_owner_in,
        ov_owner_in,
        conv_state_in,
        ov_target_in,
        ov_stiff_in,
        pd_disp_in,
        pd_pos_in,
        modulus_in,
    )
    places = (
        ov_node,
        fem_disp,
        conv_owner,
        ov_owner,
        conv_state,
        ov_target,
        ov_stiff,
        pd_disp,
        pd_pos,
        modulus,
    )
    copies = [pltpu.make_async_copy(f, t, sems.at[i]) for i, (f, t) in enumerate(zip(sources, places))]
    for copy in copies:
        copy.start()
    for copy in copies:
        copy.wait()
    _, nx, ny, nz = fem_disp.shape
    width = peers * CAP
    blocks = pd_disp.shape[1] // BLOCK
    count = ov_node.shape[1]
    node = ov_node[...]
    hot_z = one_hot(iota((nz, count), 0) == (node & (nz - 1)))
    picked = dot3(fem_disp[...].reshape(3 * nx * ny, nz), hot_z)
    hot_xy = jnp.where(iota((nx * ny, count), 0) == (node >> shift_of(nz)), 1.0, 0.0)
    at_node = jnp.sum(picked.reshape(3, nx * ny, count) * hot_xy[None], axis=1)
    conv_slot, _ = slots_of(conv_owner)
    ov_slot, ov_named = slots_of(ov_owner)
    lane = iota((conv_slot.shape[0], width), 1).astype(F32)
    state = conv_state[...]
    points = point_rows(state[0:3], state[3:6])
    blank = jnp.zeros((5, state.shape[1]), F32)
    conv_rows = jnp.concatenate([points, state[6:9], blank], axis=0)
    stiff = ov_stiff[...]
    target = ov_target[...].astype(F32)
    ov_rows = jnp.concatenate([jnp.zeros((3, count), F32), at_node, stiff, target], axis=0)
    conv_out = dot3(conv_rows, one_hot(conv_slot == lane))
    ov_out = dot3(ov_rows, one_hot(ov_slot == lane))
    pay_even[4 * blocks : 4 * blocks + 8, 0:count] = jnp.concatenate(
        [at_node, stiff, ov_named, target, node.astype(F32), jnp.zeros((1, count), F32)], axis=0
    )
    for block in range(blocks):
        for comp in range(3):
            rows_ref[comp * blocks + block : comp * blocks + block + 1] = pd_disp[
                comp : comp + 1, block * BLOCK : (block + 1) * BLOCK
            ]
    base = 3 * blocks
    for tile in range(width // BLOCK):
        part = slice(tile * BLOCK, (tile + 1) * BLOCK)
        rows_ref[base + 16 * tile : base + 16 * tile + 8] = conv_out[0:8, part]
        rows_ref[base + 16 * tile + 8 : base + 16 * tile + 16] = conv_out[8:16, part] + ov_out[:, part]
    value = rows_ref[...]
    for copy in range(chunk.shape[0]):
        chunk[copy] = value

    points = point_rows(pd_pos[...], pd_disp[...])
    for pair in range(blocks // 2):
        part = points[:, 2 * BLOCK * pair : 2 * BLOCK * (pair + 1)]
        pay_even[8 * pair : 8 * pair + 8] = part
        pay_odd[8 * pair : 8 * pair + 8] = part
    even = (lax.axis_index("lat") & 1) == 0
    for pay, top in ((pay_even, even), (pay_odd, jnp.logical_not(even))):
        row = jnp.where(top, ny - 1, 0)
        for x in range(nx):
            for comp in range(4):
                at = halo_row(4 * x + comp)
                pay[at : at + 1] = fem_disp[comp, x, pl.ds(row, 1)] if comp < 3 else modulus[x, pl.ds(row, 1)]


def halo_row(number):
    return 8 * (number // 2) + 3 + 4 * (number % 2)


def halo_rows(ref, x):
    return jnp.concatenate([ref[halo_row(4 * x + c) : halo_row(4 * x + c) + 1] for c in range(4)], axis=0)


def face_kernel(both_faces, info, fem_disp, modulus, even_side, odd_side, after, faces):
    nx, ny, nz = modulus.shape
    even = (info[0] & 1) == 0

    def rows_at(number):
        upper = halo_rows(even_side, number), halo_rows(odd_side, number)
        return jnp.where(even, upper[1], upper[0]), jnp.where(even, upper[0], upper[1])

    def put(face, chosen, low, high):
        for comp in range(4):
            faces[face, comp, 0:ny] = chosen(comp)
            faces[face, comp, ny : ny + 1] = low[comp : comp + 1]
            faces[face, comp, ny + 1 : ny + 2] = high[comp : comp + 1]

    def layer(number):
        return lambda comp: fem_disp[comp, number] if comp < 3 else modulus[number]

    if both_faces:
        for face, number in ((0, 0), (1, nx - 1)):
            put(face, layer(number), *rows_at(number))
    else:
        upper = info[1] == 0
        first, second = rows_at(nx - 1), rows_at(0)
        put(
            0,
            lambda comp: jnp.where(upper, layer(nx - 1)(comp), layer(0)(comp)),
            jnp.where(upper, first[0], second[0]),
            jnp.where(upper, first[1], second[1]),
        )


def side_table(ref, block):
    rows = ref[8 * (block // 2) : 8 * (block // 2) + 8, BLOCK * (block % 2) : BLOCK * (block % 2 + 1)]
    row = iota(rows.shape, 0)
    squares = jnp.where((row >= 4) & (row < 7), rows * rows, 0.0)
    norm = (-0.5 * LOG2E) * jnp.sum(squares, axis=0, keepdims=True)
    return jnp.where(row == 3, 1.0, jnp.where(row == 7, norm, rows))


def own_features(points):
    row = iota(points.shape, 0)
    turned = pltpu.roll(points, 4, 0)
    value = jnp.where(row == 3, turned, jnp.where(row < 3, 0.0, jnp.where(row == 7, 1.0, LOG2E * points)))
    high, mid, low = (part.astype(F32) for part in split3(value))
    return jnp.concatenate([high, mid, high, mid, low, high], axis=0).astype(BF16)


def other_features(points):
    high, mid, low = (part.astype(F32) for part in split3(points))
    left = jnp.concatenate([high, high, mid, mid, high, low], axis=0)
    sums = jnp.concatenate([high, mid, low, jnp.zeros_like(low)], axis=0)
    return left.astype(BF16).T, sums.astype(BF16)


def pair_weights(left, own):
    weight = jnp.exp2(dot(left, own))
    high = weight.astype(BF16)
    low = (weight - high.astype(F32)).astype(BF16)
    return jnp.concatenate([high, low], axis=0)


def weighted(sums, weights):
    return dot(jnp.concatenate([sums, sums], axis=1), weights)


def fold(total):
    return total[0:8] + total[8:16] + total[16:24]


def neighbours(peers, place, first, second):
    even = (place & 1) == 0
    before = jnp.where(place > 0, jnp.where(even, second, first), 0.0)
    return before, jnp.where(place < peers - 1, jnp.where(even, first, second), 0.0)


def member_codes(family, blocks, tail_blocks):
    table = blocks + tail_blocks
    side = (family >= table).astype(jnp.int32) + (family >= 2 * table).astype(jnp.int32)
    local = family - side * table
    outside = local >= blocks
    where = jnp.where(outside, 3 * blocks, side * blocks + local)
    is_tail = (outside & (family < 3 * table)).astype(jnp.int32)
    number = is_tail * (side * tail_blocks + local - blocks)
    return (((is_tail << PAIR_SHIFT) + number) << PAIR_SHIFT) + where


def low_bits(code):
    return code & ((1 << PAIR_SHIFT) - 1)


def bond_kernel(
    peers, tail_blocks, members, info, codes, own, even_side, odd_side, flat, stiffness, after, sums_out, tables, pairs, left_out, left_ref, sums_ref
):
    list_tail_pairs(flat, pairs, tail_blocks)
    left_out[...] = stiffness_rows(stiffness[...])
    blocks = sums_out.shape[0]
    mine = []
    for block in range(blocks):
        first = side_table(even_side, block)
        second = side_table(odd_side, block)
        before, following = neighbours(peers, info[0], first, second)
        mine.append(side_table(own, block))
        for side, points in enumerate((before, mine[block], following)):
            left, sums = other_features(points)
            left_ref[side * blocks + block] = left
            sums_ref[side * blocks + block] = sums
            tables[side * blocks + block] = points
    left_ref[3 * blocks] = jnp.zeros(left_ref.shape[1:], BF16)
    sums_ref[3 * blocks] = jnp.zeros(sums_ref.shape[1:], BF16)
    tables[3 * blocks] = jnp.zeros(tables.shape[1:], F32)
    totals, places, weights = {}, {}, {}
    units = blocks * members

    for unit in range(units + LAG):
        if unit < units:
            block, k = divmod(unit, members)
            if k == 0:
                features = own_features(mine[block])
            code = codes[k, block]
            places[unit] = low_bits(code)
            weights[unit] = pair_weights(left_ref[places[unit]], features)
        if unit >= LAG:
            done = unit - LAG
            block, k = divmod(done, members)
            total = weighted(sums_ref[places[done]], weights.pop(done))
            totals[block] = total if k == 0 else totals[block] + total
            if k == members - 1:
                sums_out[block] = fold(totals.pop(block))


def list_tail_pairs(flat, pairs, tail_blocks):
    row = flat[...]
    count = row.shape[1]
    slots = pairs.shape[1]
    flags = (row >> (2 * PAIR_SHIFT)).astype(F32)
    entry = (row & ((1 << (2 * PAIR_SHIFT)) - 1)).astype(F32)
    down, across = iota((count, count), 0), iota((count, count), 1)
    wide = jnp.broadcast_to(flags, (count, count))
    rank = jnp.sum(jnp.where(across < down, wide, 0.0), axis=1, keepdims=True)
    mine = jnp.sum(jnp.where(across == down, wide, 0.0), axis=1, keepdims=True)
    lane = iota((count, slots), 1).astype(F32)
    listed = dot3(entry, one_hot((rank == lane) & (mine > 0.5)))
    found = jnp.sum(flags, axis=1, keepdims=True)
    slot = iota((1, slots), 1)
    listed = jnp.where(slot.astype(F32) < found, listed, 3.0 * tail_blocks).astype(jnp.int32)
    pairs[...] = jnp.where(slot == slots - 1, found.astype(jnp.int32), listed)


def stiffness_rows(stiffness):
    new, old = iota((32, 24), 0), iota((32, 24), 1)
    place = sum(
        jnp.where(old == k, (k // 3 // 2) * 8 + (k // 3 % 2) * 4 + k % 3, 0) for k in range(24)
    )
    hot = one_hot(new == place)
    parts = [dot_nt(dot(hot, part).astype(BF16), hot) for part in split3(stiffness)]
    high, mid, low = parts
    pieces = []
    for corner in range(4):
        part = slice(8 * corner, 8 * corner + 8)
        for piece in (high, high, mid, mid, high, low):
            pieces.append(piece[:, part])
    return jnp.concatenate(pieces, axis=1).astype(BF16)


def ahead(value):
    last = value.shape[1] - 1
    return jnp.where(iota(value.shape, 1) == last, 0.0, pltpu.roll(value, last, 1))


def node_parts(node):
    row = iota(node.shape, 0)
    value = jnp.where((row != 3) & (row != 7), node, 0.0)
    high, mid, low = (part.astype(F32) for part in split3(value))
    first = jnp.concatenate([high, mid], axis=0).astype(BF16)
    return first, jnp.concatenate([low, high], axis=0).astype(BF16)


def gathered_force(total):
    turned = pltpu.roll(pltpu.roll(total, 4, 0), 1, 1)
    return total + jnp.where(iota(total.shape, 1) != 0, turned, 0.0)


def put_nodes(nodes, at, ny, fields, halves):
    for comp, value in enumerate(fields):
        shifted = ahead(value)
        for half, part in enumerate(halves):
            nodes[half, pl.ds(at + comp, ny, stride=8), :] = value[:, part]
            nodes[half, pl.ds(at + comp + 4, ny, stride=8), :] = shifted[:, part]


def take_tile(ref, at):
    return jnp.concatenate([ref[h, at : at + 8, :] for h in range(ref.shape[0])], axis=1)


def put_tile(ref, at, value):
    for half in range(ref.shape[0]):
        ref[half, at : at + 8, :] = value[:, half * BLOCK : (half + 1) * BLOCK]


def take_rows(ref, at, count):
    return jnp.concatenate([ref[h, pl.ds(at, count, stride=8), :] for h in range(ref.shape[0])], axis=1)


def rock_kernel(
    fem_disp,
    fem_vel,
    modulus,
    inv_mass,
    left_in,
    out,
    edge_nodes,
    first_ref,
    second_ref,
    nodes,
    force_ref,
):
    nx, ny, nz = modulus.shape
    halves = [slice(h * BLOCK, (h + 1) * BLOCK) for h in range(nz // BLOCK)]
    left = left_in[...]
    for x in range(nx):
        put_nodes(nodes, x * ny * 8, ny, [fem_disp[0, x], fem_disp[1, x], fem_disp[2, x], modulus[x]], halves)
    for x in range(nx):
        for y in range(ny):
            at = x * ny + y
            node = take_tile(nodes, 8 * at)
            if y in (0, ny - 1):
                edge_nodes[0 if y == 0 else 1, x] = node
            first_ref[at], second_ref[at] = node_parts(node)

    def element(x, y):
        pieces = []
        for a in range(2):
            for b in range(2):
                at = (x + a) * ny + y + b
                pieces += [first_ref[at], first_ref[at], second_ref[at]]
        return dot(left, jnp.concatenate(pieces, axis=0)) * take_tile(nodes, 8 * (x * ny + y))[3:4]

    before = None
    for x in range(nx):
        line = [element(x, y) for y in range(ny - 1)] if x < nx - 1 else None
        for y in range(ny):
            terms = []
            if line and y < ny - 1:
                terms.append(line[y][0:8])
            if line and y > 0:
                terms.append(line[y - 1][8:16])
            if before and y < ny - 1:
                terms.append(before[y][16:24])
            if before and y > 0:
                terms.append(before[y - 1][24:32])
            put_tile(force_ref, (x * ny + y) * 8, gathered_force(sum(terms[1:], terms[0])))
        before = line
    for x in range(nx):
        for comp in range(3):
            force = take_rows(force_ref, x * ny * 8 + comp, ny)
            out[comp, x] = fem_vel[comp, x] - HALF * inv_mass[x] * force


def outer_kernel(
    depth,
    info,
    rock,
    inv_mass,
    modulus,
    left_in,
    first_in,
    second_in,
    low_x,
    high_x,
    after,
    out,
    edge_nodes,
    nodes,
    first_ref,
    second_ref,
    force_ref,
):
    nx, ny, nz = inv_mass.shape
    halves = [slice(h * BLOCK, (h + 1) * BLOCK) for h in range(nz // BLOCK)]
    left = left_in[...]
    on = (jnp.where(info[1] > 0, 1.0, 0.0), jnp.where(info[1] < depth - 1, 1.0, 0.0))
    for side, face in enumerate((low_x, high_x)):
        put_nodes(nodes, side * ny * 8, ny, [face[comp, 0:ny] * on[side] for comp in range(4)], halves)
    for side in range(2):
        for y in range(ny):
            at = side * ny + y
            node = take_tile(nodes, 8 * at)
            if y in (0, ny - 1):
                edge_nodes[0 if y == 0 else 1, side] = node
            first_ref[at], second_ref[at] = node_parts(node)

    def inner(y, side):
        at = (nx - 1 if side else 0) * ny + y
        return first_in[at], second_in[at]

    def outer(y, side):
        return first_ref[side * ny + y], second_ref[side * ny + y]

    for side in range(2):
        line = []
        for y in range(ny - 1):
            pieces = []
            for a in range(2):
                for b in range(2):
                    first, second = (inner if a != side else outer)(y + b, side)
                    pieces += [first, first, second]
            mod = modulus[nx - 1, y : y + 1] if side else take_tile(nodes, 8 * y)[3:4]
            line.append(dot(left, jnp.concatenate(pieces, axis=0)) * mod)
        start = 0 if side else 16
        for y in range(ny):
            terms = []
            if y < ny - 1:
                terms.append(line[y][start : start + 8])
            if y > 0:
                terms.append(line[y - 1][start + 8 : start + 16])
            put_tile(force_ref, (side * ny + y) * 8, gathered_force(sum(terms[1:], terms[0])))
    for x in range(nx):
        for comp in range(3):
            value = rock[comp, x]
            if x in (0, nx - 1):
                side = 0 if x == 0 else 1
                value = value - HALF * inv_mass[x] * take_rows(force_ref, side * ny * 8 + comp, ny)
            out[comp, x] = value


def received(ref, peers, blocks, place, odd, wanted, row, pick):
    width = peers * CAP
    base = 3 * blocks

    def slot_rows(k):
        tiles = [ref[k, base + 16 * t : base + 16 * t + 16, :] for t in range(width // BLOCK)]
        return tiles[0] if len(tiles) == 1 else jnp.concatenate(tiles, axis=1)

    lane = iota((16, width), 1)
    back = lax.rem(width - CAP * (place - 1) + width, width)
    gathered = [jnp.zeros((16, width), F32) for _ in range(3)]
    for k in range(peers // 2):
        turned = pltpu.roll(slot_rows(k), back, 1)
        for side in range(3):
            window = jnp.where((lane >= CAP * side) & (lane < CAP * side + CAP), turned, 0.0)
            amount = (2 * CAP * k - CAP * side) % width
            gathered[side] = gathered[side] + (pltpu.roll(window, amount, 1) if amount else window)
    tails = [pltpu.roll(part, CAP * odd, 1) for part in gathered]
    rows = peers // 2 * blocks
    hit = (iota((rows, pick.shape[1]), 0) == row) & wanted
    looked = dot3(ref[:, 0:base, :].reshape(peers // 2 * base, BLOCK), pick)
    looked = looked.reshape(peers // 2, base, pick.shape[1])
    values = []
    for comp in range(3):
        got = looked[:, comp * blocks : (comp + 1) * blocks, :].reshape(rows, pick.shape[1])
        values.append(jnp.sum(jnp.where(hit, got, 0.0), axis=0, keepdims=True))
    return tails, values


def entry_rows(side, blocks, count):
    return side[4 * blocks : 4 * blocks + 8, 0:count]


def entry_places(entry, blocks):
    owner = entry[4:5].astype(jnp.int32)
    goal = entry[5:6].astype(jnp.int32)
    pick = one_hot(iota((BLOCK, entry.shape[1]), 0) == (goal & (BLOCK - 1)))
    return owner & 1, (owner >> 1) * blocks + (goal >> shift_of(BLOCK)), pick


def edge_kernel(
    peers,
    depth,
    blocks,
    info,
    mine_in,
    own_side,
    rock,
    inv_mass,
    edge_nodes,
    outer_nodes,
    left_in,
    low_x,
    high_x,
    even_side,
    odd_side,
    out,
    tails_out,
    values_out,
):
    nx, ny, nz = inv_mass.shape
    place = info[0]
    core = place & 1
    even = core == 0
    entry = entry_rows(own_side, blocks, values_out.shape[1])
    odd_owner, row, pick = entry_places(entry, blocks)
    tails, values = received(mine_in, peers, blocks, place, core, odd_owner == core, row, pick)
    for side in range(3):
        tails_out[side] = tails[side]
    values_out[...] = jnp.concatenate(values + [jnp.zeros((5, entry.shape[1]), F32)], axis=0)

    left = left_in[...]
    low_on = jnp.where(info[1] > 0, 1.0, 0.0)
    high_on = jnp.where(info[1] < depth - 1, 1.0, 0.0)
    for edge, from_even, node_y in ((0, jnp.logical_not(even), 0), (1, even, ny - 1)):
        inner, outer, lower = [], [], []
        for x in range(nx + 2):
            if x == 0:
                value = low_x[:, ny + edge] * low_on
            elif x == nx + 1:
                value = high_x[:, ny + edge] * high_on
            else:
                value = jnp.where(from_even, halo_rows(even_side, x - 1), halo_rows(odd_side, x - 1))
            other = jnp.concatenate([value, ahead(value)], axis=0)
            node = outer_nodes[edge, x // (nx + 1)] if x in (0, nx + 1) else edge_nodes[edge, x - 1]
            lower.append((other if edge == 0 else node)[3:4])
            inner.append(node_parts(node))
            outer.append(node_parts(other))
        forces = []
        for x in range(nx + 1):
            pieces = []
            for a in range(2):
                for b in range(2):
                    first, second = (outer if (b == 0) == (edge == 0) else inner)[x + a]
                    pieces += [first, first, second]
            forces.append(dot(left, jnp.concatenate(pieces, axis=0)) * lower[x])
        start = 8 if edge == 0 else 0
        for x in range(nx):
            total = forces[x + 1][start : start + 8] + forces[x][start + 16 : start + 24]
            force = gathered_force(total)
            rest = slice(1, ny - 1)
            for comp in range(3):
                scaled = HALF * inv_mass[x, node_y : node_y + 1] * force[comp : comp + 1]
                out[comp, x, node_y : node_y + 1] = rock[comp, x, node_y : node_y + 1] - scaled
                if edge == 0:
                    out[comp, x, rest] = rock[comp, x, rest]


def final_kernel(
    peers,
    members,
    info,
    pairs,
    codes,
    mate_in,
    own_side,
    rock,
    inv_mass,
    tails_in,
    values_in,
    sums_in,
    tables,
    pd_vel,
    fem_out,
    pd_out,
    sums_ref,
    own,
    tail_left,
    tail_sums,
):
    nx, ny, nz = inv_mass.shape
    width = peers * CAP
    tail_blocks = width // BLOCK
    blocks = sums_in.shape[0]
    table = blocks + tail_blocks
    place = info[0]
    core = place & 1
    for block in range(blocks):
        sums_ref[block] = sums_in[block]
        own[block] = tables[blocks + block]

    count = values_in.shape[1]
    entry = entry_rows(own_side, blocks, count)
    odd_owner, row, pick = entry_places(entry, blocks)
    tails, values = received(mate_in, peers, blocks, place, 1 - core, odd_owner != core, row, pick)
    tails = [tails[side] + tails_in[side] for side in range(3)]
    on = (jnp.where(place > 0, 1.0, 0.0), 1.0, jnp.where(place < peers - 1, 1.0, 0.0))
    for side in range(3):
        for tile in range(tail_blocks):
            points = tails[side][0:8, tile * BLOCK : (tile + 1) * BLOCK] * on[side]
            tail_left[side * tail_blocks + tile], tail_sums[side * tail_blocks + tile] = other_features(points)
            if side == 1:
                own[blocks + tile] = points
    tail_left[3 * tail_blocks] = jnp.zeros(tail_left.shape[1:], BF16)
    tail_sums[3 * tail_blocks] = jnp.zeros(tail_sums.shape[1:], BF16)
    tail_rows = tails[1]

    for tile in range(tail_blocks):
        block = blocks + tile
        features = own_features(own[block])
        ready = []
        for k in range(members):
            left, rows = other_features(tables[low_bits(codes[k, block])])
            ready.append((rows, pair_weights(left, features)))
        results = [weighted(rows, weights) for rows, weights in ready]
        sums_ref[block] = fold(sum(results[1:], results[0]))

    def some(index, carry):
        ready = []
        for k in range(BATCH):
            code = pairs[0, BATCH * index + k]
            block, number = code >> PAIR_SHIFT, low_bits(code)
            weights = pair_weights(tail_left[number], own_features(own[block]))
            ready.append((block, tail_sums[number], weights))
        results = [(block, fold(weighted(rows, weights))) for block, rows, weights in ready]
        for block, total in results:
            sums_ref[block] = sums_ref[block] + total
        return carry

    node = entry[6:7].astype(jnp.int32)
    z_hot = one_hot(iota((nz, count), 0) == (node & (nz - 1)))
    xy_hit = iota((nx * ny, count), 0) == (node >> shift_of(nz))
    spread = []
    for comp in range(3):
        value = values[comp] + values_in[comp : comp + 1]
        spread.append(jnp.where(xy_hit, entry[3:4] * (entry[comp : comp + 1] - value), 0.0))
    pull = dot3_nt(jnp.concatenate(spread, axis=0), z_hot).reshape(3, nx, ny, nz)
    fem_out[...] = rock[...] - HALF * inv_mass[...][None] * pull

    stiff = tail_rows[14:15]
    target = tail_rows[15:16].astype(jnp.int32)
    hot_lane = one_hot(iota((BLOCK, width), 0) == (target & (BLOCK - 1)))
    target_block = target >> shift_of(BLOCK)
    looked = dot3(tables[blocks : 2 * blocks].reshape(blocks * 8, BLOCK), hot_lane)
    found = jnp.zeros((8, width), F32)
    for block in range(blocks):
        found = found + jnp.where(target_block == block, looked[8 * block : 8 * block + 8], 0.0)
    coupling = stiff * (tail_rows[11:14] - found[0:3])
    coupling = jnp.concatenate([coupling, jnp.zeros((5, width), F32)], axis=0)
    spread = jnp.concatenate([jnp.where(target_block == block, coupling, 0.0) for block in range(blocks)], axis=0)
    couple = dot3_nt(spread, hot_lane)

    lax.fori_loop(0, (pairs[0, PAIR_SLOTS - 1] + BATCH - 1) // BATCH, some, 0)

    scale = GAIN / (BLOCK * members)
    for block in range(table):
        total = sums_ref[block]
        points = own[block]
        part = slice(block * BLOCK, (block + 1) * BLOCK)
        force = scale * points[3:4] * (total[0:3] - points[0:3] * total[3:4])
        if block < blocks:
            pd_out[:, part] = pd_vel[:, part] + HALF * (force + couple[8 * block : 8 * block + 3])
        else:
            tile = block - blocks
            pd_out[:, part] = tail_rows[8:11, tile * BLOCK : (tile + 1) * BLOCK] + HALF * force


def call(kernel, outs, specs, scratch, microseconds, args, name, out_specs=None, vmem=24):
    return pl.pallas_call(
        kernel,
        out_shape=outs,
        in_specs=specs,
        out_specs=out_specs or jax.tree.map(lambda _: VMEM, outs),
        scratch_shapes=scratch,
        compiler_params=params(vmem),
        cost_estimate=pl.CostEstimate(flops=0, bytes_accessed=int(3.6e6 * microseconds), transcendentals=0),
        name=name,
    )(*args)


def shards(
    fem_disp,
    fem_vel,
    modulus,
    inv_mass,
    element_stiffness,
    pd_pos,
    pd_disp,
    pd_vel,
    conv_state,
    conv_owner,
    family,
    ov_owner,
    ov_node,
    ov_target,
    ov_stiff,
):
    peers = lax.axis_size("lat")
    depth = lax.axis_size("depth")
    nx, ny, nz = modulus.shape
    blocks = pd_pos.shape[1] // BLOCK
    tail_blocks = peers * CAP // BLOCK
    table = blocks + tail_blocks
    members = family.shape[1]
    count = ov_node.shape[0]
    chips = peers // 2
    chunk_rows = 3 * blocks + 16 * tail_blocks
    shaped = jax.ShapeDtypeStruct
    info = jnp.stack([lax.axis_index("lat"), lax.axis_index("depth")]).astype(jnp.int32)

    both_faces = depth > 2
    family = family.T
    inputs = (
        ov_node.reshape(1, -1),
        fem_disp,
        conv_owner.reshape(1, -1),
        ov_owner.reshape(1, -1),
        conv_state,
        ov_target.reshape(1, -1),
        ov_stiff.reshape(1, -1),
        pd_disp,
        pd_pos,
        modulus,
    )
    chunk, pay_even, pay_odd = call(
        functools.partial(pack_kernel, peers),
        (
            shaped((chips, chunk_rows, BLOCK), F32),
            shaped((4 * blocks + 8, nz), F32),
            shaped((4 * blocks, nz), F32),
        ),
        [FAR] * 10,
        [pltpu.VMEM((chunk_rows, BLOCK), F32)]
        + [pltpu.VMEM(value.shape, value.dtype) for value in inputs]
        + [pltpu.SemaphoreType.DMA((10,))],
        2.6,
        inputs,
        "pack",
        vmem=SIDE_VMEM,
    )
    swap = [(i, i ^ 1) for i in range(peers)]
    cross = [(i, i + 1) for i in range(1, peers - 1, 2)] + [(i + 1, i) for i in range(1, peers - 1, 2)]
    odd_side = lax.ppermute(pay_odd, "lat", cross)
    even_side = lax.ppermute(pay_even, "lat", swap)
    groups = [[side + 2 * k for k in range(chips)] for side in range(2)]
    mine = lax.all_to_all(chunk, "lat", split_axis=0, concat_axis=0, tiled=True, axis_index_groups=groups)

    node_count = nx * ny
    codes = member_codes(family, blocks, tail_blocks)
    block_of = jnp.arange(table, dtype=jnp.int32)[None, :]
    flat = codes >> PAIR_SHIFT
    flat = ((flat >> PAIR_SHIFT) << (2 * PAIR_SHIFT)) + (block_of << PAIR_SHIFT) + low_bits(flat)
    count_faces = 2 if both_faces else 1
    rows = jnp.stack([even_side[: 4 * blocks], odd_side]).reshape(2, blocks // 2, 2, 4, nz)[:, :, :, 3]
    rows = rows.reshape(2, blocks, nz)[:, : 4 * nx].reshape(2, nx, 4, nz)
    even = (info[0] & 1) == 0
    ends = jnp.stack([jnp.where(even, rows[1], rows[0]), jnp.where(even, rows[0], rows[1])], axis=2)
    own = jnp.concatenate([fem_disp, modulus[None]], axis=0)
    layers = [jnp.concatenate([own[:, x], ends[x]], axis=1) for x in (0, nx - 1)]
    if both_faces:
        faces = jnp.stack(layers)
    else:
        faces = jnp.where(info[1] == 0, layers[1], layers[0])[None]
    faces, pay_even, even_side, odd_side = lax.optimization_barrier((faces, pay_even, even_side, odd_side))
    if both_faces:
        low_x = lax.ppermute(faces[1], "depth", [(i, i + 1) for i in range(depth - 1)])
        high_x = lax.ppermute(faces[0], "depth", [(i + 1, i) for i in range(depth - 1)])
    else:
        low_x = high_x = lax.ppermute(faces[0], "depth", [(0, 1), (1, 0)])

    sums, tables, pairs, left = call(
        functools.partial(bond_kernel, peers, tail_blocks, members),
        (
            shaped((blocks, 8, BLOCK), F32),
            shaped((3 * blocks + 1, 8, BLOCK), F32),
            shaped((1, PAIR_SLOTS), jnp.int32),
            shaped((32, 192), BF16),
        ),
        [SMEM, SMEM] + [VMEM] * 5 + [ANY],
        [pltpu.VMEM((3 * blocks + 1, BLOCK, 48), BF16), pltpu.VMEM((3 * blocks + 1, 32, BLOCK), BF16)],
        4.3,
        (info, codes, pay_even, even_side, odd_side, flat.reshape(1, -1), element_stiffness, faces),
        "bond",
    )
    rock, edge_nodes, first_parts, second_parts = call(
        rock_kernel,
        (
            shaped(fem_vel.shape, F32),
            shaped((2, nx, 8, nz), F32),
            shaped((node_count, 16, nz), BF16),
            shaped((node_count, 16, nz), BF16),
        ),
        [VMEM] * 5,
        [
            pltpu.VMEM((nz // BLOCK, node_count * 8, BLOCK), F32),
            pltpu.VMEM((nz // BLOCK, node_count * 8, BLOCK), F32),
        ],
        1.2,
        (fem_disp, fem_vel, modulus, inv_mass, left),
        "rock",
    )
    mine, sums, low_x, high_x = lax.optimization_barrier((mine, sums, low_x, high_x))
    mate = lax.ppermute(mine, "lat", swap)
    rock, outer_nodes = call(
        functools.partial(outer_kernel, depth),
        (shaped(fem_vel.shape, F32), shaped((2, 2, 8, nz), F32)),
        [SMEM] + [VMEM] * 8 + [ANY],
        [
            pltpu.VMEM((nz // BLOCK, 2 * ny * 8, BLOCK), F32),
            pltpu.VMEM((2 * ny, 16, nz), BF16),
            pltpu.VMEM((2 * ny, 16, nz), BF16),
            pltpu.VMEM((nz // BLOCK, 2 * ny * 8, BLOCK), F32),
        ],
        0.8,
        (info, rock, inv_mass, modulus, left, first_parts, second_parts, low_x, high_x, sums),
        "outer",
    )
    rock, tails, values = call(
        functools.partial(edge_kernel, peers, depth, blocks),
        (shaped(fem_vel.shape, F32), shaped((3, 16, peers * CAP), F32), shaped((8, count), F32)),
        [SMEM] + [VMEM] * 11,
        [],
        1.0,
        (info, mine, pay_even, rock, inv_mass, edge_nodes, outer_nodes, left, low_x, high_x, even_side, odd_side),
        "edge",
    )
    return call(
        functools.partial(final_kernel, peers, members),
        (shaped(fem_vel.shape, F32), shaped((3, table * BLOCK), F32)),
        [SMEM] * 3 + [VMEM] * 9,
        [
            pltpu.VMEM((table, 8, BLOCK), F32),
            pltpu.VMEM((table, 8, BLOCK), F32),
            pltpu.VMEM((3 * tail_blocks + 1, BLOCK, 48), BF16),
            pltpu.VMEM((3 * tail_blocks + 1, 32, BLOCK), BF16),
        ],
        2.6,
        (info, pairs, codes, mate, pay_even, rock, inv_mass, tails, values, sums, tables, pd_vel),
        "final",
    )


def solution(mesh):
    lat = P(None, ("depth", "lat"))
    rows = P(("depth", "lat"), None)
    flat = P(("depth", "lat"))
    nodes = P(None, "depth", "lat", None)
    grid = P("depth", "lat", None)
    return jax.shard_map(
        shards,
        mesh=mesh,
        in_specs=(nodes, nodes, grid, grid, P(), lat, lat, lat, lat, rows, rows, rows, flat, flat, flat),
        out_specs=(nodes, lat),
        check_vma=False,
    )
```
